256 devices in a mesh: dom: 32 (over x, z), col: 8 (over y, core).
Axes of the slice: x: 4, y: 4, z: 8, core: 2. Of those that a mesh axis runs over, the one named last changes fastest.
Arguments:
- band_tiles: float32 [6144, 128, 128], P(('dom', 'col')), may hold values from -0.1875 to 0.1875
- band_rows: int32 [6144], P(('dom', 'col')), may hold values from 0 to 31
- band_cols: int32 [6144], P(('dom', 'col')), may hold values from 0 to 47
- hub_tiles: float32 [2048, 128, 128], P(('dom', 'col')), may hold values from -0.1875 to 0.1875
- hub_rows: int32 [2048], P(('dom', 'col')), may hold values from 0 to 31
- hub_slots: int32 [2048], P(('dom', 'col')), may hold values from 0 to 31
- hub_blocks: int32 [32], replicated, may hold values from 0 to 1023, as said below
- start_vectors: float32 [131072, 64], P(('dom', 'col'))
- prior_directions: float32 [131072, 64], P(('dom', 'col'))
- rotation: float32 [2, 192, 64], replicated, as said below
Outputs:
- final_vectors: float32 [131072, 64], P(('dom', 'col'))
- final_directions: float32 [131072, 64], P(('dom', 'col'))
- ritz_block: float32 [64, 64], replicated
The draws below stay inside these ranges and needn't reach their ends.
Inputs may be any that keep to these rules, and one draw needn't show every extreme that they name: hub_blocks[p] lies in panel p, between p * 32 and p * 32 + 31. Each rotation[i] has full column rank.
All inputs are finite; a program needn't handle non-finite values.
Results may differ from the reference program's by a relative error of at most 0.0034.
Values sent between devices are 32-bit elements; how exact they have to be, the bound alone decides.
A program may use at most 64 MiB of HBM per device.

```python
import jax
import jax.numpy as jnp
from jax import lax

TB = 128
K = 64
PB = 32
TPD = 24
HTD = 8
ITERS = 2
HW = 8
HUBS = 32
ROWS = 131072
TILES = 6144
HTILES = 2048
N_DOM = 32
N_COL = 8


def scaled_rows(key):
    row_key, entry_key = jax.random.split(key, 2)
    scales = jnp.exp(jax.random.uniform(row_key, (ROWS, 1), jnp.float32) * 2.302585)
    base = jax.random.normal(entry_key, (ROWS, K), jnp.float32)
    return base * scales / jnp.sqrt(22.0 * ROWS)


def draw_start_vectors(key, part):
    key = jax.random.fold_in(key, 11)
    return scaled_rows(key)


def draw_prior_directions(key, part):
    key = jax.random.fold_in(key, 12)
    return 0.7 * scaled_rows(key)


def draw_rotation(key, part):
    key = jax.random.fold_in(key, 13)
    top_key, rest_key = jax.random.split(key)
    top = 0.3 * jax.random.normal(top_key, (ITERS, K, K), jnp.float32)
    rest = 0.5 * jax.random.normal(rest_key, (ITERS, 2 * K, K), jnp.float32)
    top = top / jnp.sqrt(1.0 * K) + jnp.eye(K, dtype=jnp.float32)[None]
    rest = rest / jnp.sqrt(1.0 * K)
    return jnp.concatenate([top, rest], axis=1)


def draw_hub_blocks(key, part):
    key = jax.random.fold_in(key, 14)
    local_rows = jax.random.randint(key, (N_DOM,), 0, PB, jnp.int32)
    return jnp.arange(N_DOM, dtype=jnp.int32) * PB + local_rows


def plant(array, rng, smallest, high):
    extent = array.shape
    spot = [jax.random.randint(jax.random.fold_in(rng, axis), (), 0, extent[axis]) for axis in range(len(extent))]
    array = array.at[tuple(spot)].set(smallest)
    longest = extent.index(max(extent))
    spot[longest] = (spot[longest] + 1) % extent[longest]
    return array.at[tuple(spot)].set(high)


def levels(key, dims, cuts, smallest, top_value):
    loudness = 1.0
    for axis_at, blocks in cuts:
        steps = jax.random.uniform(jax.random.fold_in(jax.random.fold_in(key, 6), axis_at), (blocks,), jnp.float32, smallest / len(cuts), top_value / len(cuts))
        loudness = loudness * jnp.repeat(jnp.exp(steps), dims[axis_at] // blocks).reshape((-1,) + (1,) * (len(dims) - 1 - axis_at))
    return loudness


def centred(key, extent, spread, bound, cuts=(), kind=jnp.bfloat16):
    factor_of = levels(key, extent, cuts, -0.22, 0.18) if cuts else 1.0
    entries = jax.random.normal(key, extent, jnp.float32) * spread * factor_of
    return jnp.minimum(jnp.maximum(entries, -bound), bound).astype(kind)


def setup_inputs(seed: int = 0) -> dict:
    splits = jax.random.split(jax.random.key(seed), 11)
    band_tiles = centred(splits[0], (TILES, TB, TB), (TB * (TPD + HTD) * N_COL // PB) ** -0.5, 0.1875, ((0, 256),), jnp.float32)
    band_rows = plant(jax.random.randint(splits[1], (TILES,), 0, PB), jax.random.fold_in(splits[1], 1), 0, PB - 1).astype(jnp.int32)
    band_cols = plant(jax.random.randint(splits[2], (TILES,), 0, PB + 2 * HW), jax.random.fold_in(splits[2], 1), 0, (PB + 2 * HW) - 1).astype(jnp.int32)
    hub_tiles = centred(splits[3], (HTILES, TB, TB), (TB * (TPD + HTD) * N_COL // PB) ** -0.5, 0.1875, ((0, 256),), jnp.float32)
    hub_rows = plant(jax.random.randint(splits[4], (HTILES,), 0, PB), jax.random.fold_in(splits[4], 1), 0, PB - 1).astype(jnp.int32)
    hub_slots = plant(jax.random.randint(splits[5], (HTILES,), 0, HUBS), jax.random.fold_in(splits[5], 1), 0, HUBS - 1).astype(jnp.int32)
    hub_blocks = draw_hub_blocks(jax.random.fold_in(splits[10], 71), 0)
    start_vectors = draw_start_vectors(jax.random.fold_in(splits[10], 71), 0)
    prior_directions = draw_prior_directions(jax.random.fold_in(splits[10], 71), 0)
    rotation = draw_rotation(jax.random.fold_in(splits[10], 71), 0)
    return {"band_tiles": band_tiles, "band_rows": band_rows, "band_cols": band_cols, "hub_tiles": hub_tiles, "hub_rows": hub_rows, "hub_slots": hub_slots, "hub_blocks": hub_blocks, "start_vectors": start_vectors, "prior_directions": prior_directions, "rotation": rotation}


def apply_graph(vectors, band_tiles, band_rows, band_cols, hub_tiles, hub_rows, hub_slots, hub_blocks):
    columns = vectors.shape[1]
    blocks = vectors.reshape(N_DOM, PB, TB, columns)
    hub_vectors = vectors.reshape(N_DOM * PB, TB, columns)[hub_blocks]
    band_set = band_tiles.reshape(N_DOM, N_COL * TPD, TB, TB)
    band_row_set = band_rows.reshape(N_DOM, N_COL * TPD)
    band_col_set = band_cols.reshape(N_DOM, N_COL * TPD)
    hub_set = hub_tiles.reshape(N_DOM, N_COL * HTD, TB, TB)
    hub_row_set = hub_rows.reshape(N_DOM, N_COL * HTD)
    hub_slot_set = hub_slots.reshape(N_DOM, N_COL * HTD)

    def panel_step(position):
        before = blocks[(position - 1) % N_DOM][PB - HW:]
        after = blocks[(position + 1) % N_DOM][:HW]
        extended = jnp.concatenate([before, blocks[position], after], axis=0)
        picked = extended[band_col_set[position]]
        products = jnp.einsum('tij,tjc->tic', band_set[position], picked, precision=lax.Precision.HIGHEST)
        result = jax.ops.segment_sum(products, band_row_set[position], PB)
        hub_picked = hub_vectors[hub_slot_set[position]]
        hub_products = jnp.einsum('tij,tjc->tic', hub_set[position], hub_picked, precision=lax.Precision.HIGHEST)
        return result + jax.ops.segment_sum(hub_products, hub_row_set[position], PB)
    outputs = lax.map(panel_step, jnp.arange(N_DOM, dtype=jnp.int32))
    return outputs.reshape(N_DOM * PB * TB, columns)

def rotate(basis, gram_matrix, coeffs):
    highest = lax.Precision.HIGHEST
    reduced = jnp.dot(jnp.dot(coeffs.T, gram_matrix, precision=highest), coeffs, precision=highest)
    factor = jnp.linalg.cholesky(reduced)
    identity = jnp.eye(K, dtype=reduced.dtype)
    inverse = lax.linalg.triangular_solve(factor, identity, left_side=True, lower=True)
    new_vectors = jnp.dot(jnp.dot(basis, coeffs, precision=highest), inverse.T, precision=highest)
    new_directions = jnp.dot(jnp.dot(basis[:, K:], coeffs[K:], precision=highest), inverse.T, precision=highest)
    return (new_vectors, new_directions)

def reference(band_tiles, band_rows, band_cols, hub_tiles, hub_rows, hub_slots, hub_blocks, start_vectors, prior_directions, rotation):
    highest = lax.Precision.HIGHEST
    vectors, directions = (start_vectors, prior_directions)
    ritz_block = jnp.zeros((K, K), start_vectors.dtype)
    for step in range(ITERS):
        image = vectors - apply_graph(vectors, band_tiles, band_rows, band_cols, hub_tiles, hub_rows, hub_slots, hub_blocks)
        ritz_block = jnp.dot(vectors.T, image, precision=highest)
        residual = image - jnp.dot(vectors, ritz_block, precision=highest)
        basis = jnp.concatenate([vectors, residual, directions], axis=1)
        gram_matrix = jnp.dot(basis.T, basis, precision=highest)
        vectors, directions = rotate(basis, gram_matrix, rotation[step])
    return (vectors, directions, ritz_block)
```

```python
import jax
import jax.numpy as jnp
from jax import lax
from jax.experimental import pallas as pl
from jax.experimental.pallas import tpu as pltpu
from jax.sharding import PartitionSpec as P

TB = 128
K = 64
PB = 32
ITERS = 2
HW = 8
NZ = 8
NX = 4
NY = 4
N_DOM = 32
N_COL = 8
TPD = 24
HTD = 8
NT = TPD + HTD
OWN = 4
EXT = PB + 2 * HW
HUBS = 32
MESH = pl.DeviceIdType.MESH
F32 = jnp.float32
BF16 = jnp.bfloat16
HI = lax.Precision.HIGHEST


def wrap(value, count):
    return lax.rem(value + count, count)


def nn(a, b):
    return jnp.dot(a, b, precision=HI, preferred_element_type=F32)


def nt(a, b):
    return lax.dot_general(a, b, (((1,), (1,)), ((), ())), precision=HI, preferred_element_type=F32)


def split(value):
    high = value.astype(BF16)
    return high, (value - high.astype(F32)).astype(BF16)


def eliminate(matrix):
    rows = lax.broadcasted_iota(jnp.int32, (8, 2 * K), 0)
    lanes = lax.broadcasted_iota(jnp.int32, (8, 2 * K), 1)
    wide = jnp.concatenate([matrix, jnp.zeros((K, K), F32)], axis=1)
    blocks = [
        jnp.where(lanes - K == rows + 8 * b, 1.0, wide[8 * b : 8 * b + 8]) for b in range(K // 8)
    ]
    for k in range(K):
        home = k // 8
        row = jnp.broadcast_to(blocks[home][k % 8 : k % 8 + 1, :], (8, 2 * K))
        pivot = jnp.broadcast_to(row[:, k : k + 1], (8, 2 * K))
        scaled = row / pivot
        for b in range(home, K // 8):
            column = jnp.broadcast_to(blocks[b][:, k : k + 1], (8, 2 * K))
            if b == home:
                column = jnp.where(rows > k % 8, column, 0.0)
                own = row * lax.rsqrt(pivot)
                blocks[b] = jnp.where(rows == k % 8, own, blocks[b] - column * scaled)
            else:
                blocks[b] = blocks[b] - column * scaled
    return jnp.concatenate(blocks, axis=0)[:, K:]


def kernel(
    idx, flt, vec_in, dir_in, rot, band_hbm, hub_hbm,
    vec_out, dir_out, ritz_out,
    tiles, weights, state, image, own, ext, cand, hca, hubx, prods, ssend, srecv, rsum, rrecv,
    pay, ra, rb1, rb2, rcbuf, tsum, lsem, ssem, rsem,
):
    d = lax.axis_index("dom")
    q = lax.axis_index("col")
    x, z = d // NZ, d % NZ
    y, c = q // 2, q % 2
    sib = (d, q + 1 - 2 * c)

    def at_y(k):
        return (d, 2 * wrap(y + k, NY) + c)

    def at_xz(i, k):
        return (wrap(x + i, NX) * NZ + wrap(z + k, NZ), q)

    cols = [(d, wrap(q + k, N_COL)) for k in range(1, N_COL)]
    others = [(i, k) for i in range(NX) for k in range(NZ) if (i, k) != (0, 0)]
    partners = cols + [at_xz(i, k) for i, k in others]

    barrier = pltpu.get_barrier_semaphore()
    for partner in partners:
        pl.semaphore_signal(barrier, inc=1, device_id=partner, device_id_type=MESH)

    band_copy = pltpu.make_async_copy(band_hbm, tiles.at[pl.ds(0, TPD)], lsem.at[0])
    hub_copy = pltpu.make_async_copy(hub_hbm, tiles.at[pl.ds(TPD, HTD)], lsem.at[1])
    band_copy.start()
    hub_copy.start()
    state[0:K] = vec_in[...]
    state[K:] = dir_in[...]
    band_copy.wait()
    hub_copy.wait()

    def prepare(t, carry):
        high, low = split(tiles[t].T)
        weights[t, 0:TB] = high
        weights[t, TB:] = low
        return carry

    lax.fori_loop(0, NT, prepare, 0)
    pl.semaphore_wait(barrier, len(partners))

    def step(it, carry):
        counts = {"s": 0, "r": 0}

        def sems(n=1):
            s, r = counts["s"], counts["r"]
            counts["s"] += n
            counts["r"] += n
            return s

        def send(src, dst, sem, device):
            copy = pltpu.make_async_remote_copy(
                src_ref=src, dst_ref=dst, send_sem=ssem.at[it, sem], recv_sem=rsem.at[it, sem],
                device_id=device, device_id_type=MESH,
            )
            copy.start()
            return copy

        def arrived(ref, sem):
            pltpu.make_async_copy(ref, ref, rsem.at[it, sem]).wait()

        def sent(ref, sem):
            pltpu.make_async_copy(ref, ref, ssem.at[it, sem]).wait()

        pending = []

        pick = jnp.zeros((K, TB), F32)
        for j in range(OWN):
            block = state[0:K, TB * j : TB * (j + 1)]
            own[it, j] = block
            ext[it, HW + OWN * q + j] = block
            pick = pick + block * flt[2 * NT + j]
        cand[it] = pick

        g_ha = sems()
        for k in range(1, N_COL):
            peer = wrap(q + k, N_COL)
            send(cand.at[it, pl.ds(8 * peer, 8)], hca.at[it, q], g_ha, (d, peer))
        pending.append((hca.at[it, pl.ds(0, N_COL - 1)], g_ha))
        hca[it, q] = cand[it, pl.ds(8 * q, 8)]

        g_p = sems(NY)
        mine = ext.at[it, pl.ds(HW + OWN * q, OWN)]
        for k in (1, 3, 2):
            pending.append(send(own.at[it], mine, g_p + k, at_y(k)))
        pending.append(send(own.at[it], mine, g_p, sib))

        arrived(hca.at[it, pl.ds(0, N_COL - 1)], g_ha)
        piece = hca[it, 0]
        for k in range(1, N_COL):
            piece = piece + hca[it, k]
        hubx[it, d] = piece
        g_hb = sems()
        for i, k in others:
            send(hubx.at[it, d], hubx.at[it, d], g_hb, at_xz(i, k))
        pending.append((hubx.at[it, pl.ds(0, N_DOM - 1)], g_hb))

        g_pf = sems(NY)
        for k in (1, 3, 2):
            block = ext.at[it, pl.ds(HW + OWN * (2 * wrap(y - k, NY) + c), OWN)]
            arrived(block, g_p + k)
            pending.append(send(block, block, g_pf + k, sib))
        g_h = sems(4)
        low, high = pl.ds(OWN * c, OWN), pl.ds(HW + PB + OWN * c, OWN)
        pending.append(
            send(ext.at[it, pl.ds(HW + OWN * (N_COL - 2 + c), OWN)], ext.at[it, low], g_h, (wrap(d + 1, N_DOM), q))
        )
        pending.append(
            send(ext.at[it, pl.ds(HW + OWN * c, OWN)], ext.at[it, high], g_h + 1, (wrap(d - 1, N_DOM), q))
        )

        arrived(hubx.at[it, pl.ds(0, N_DOM - 1)], g_hb)
        g_c = sems(NY)
        mine = ext.at[it, pl.ds(EXT, HUBS), pl.ds(8 * q, 8)]
        for k in (1, 3, 2):
            pending.append(send(hubx.at[it], mine, g_c + k, at_y(k)))
        pending.append(send(hubx.at[it], mine, g_c, sib))
        for s in range(HUBS):
            ext[it, EXT + s, pl.ds(8 * q, 8)] = hubx[it, s]

        for n, part in enumerate((low, high)):
            arrived(ext.at[it, part], g_h + n)
            pending.append(send(ext.at[it, part], ext.at[it, part], g_h + 2 + n, sib))
        g_cf = sems(NY)
        for k in (1, 3, 2):
            part = ext.at[it, pl.ds(EXT, HUBS), pl.ds(8 * (2 * wrap(y - k, NY) + c), 8)]
            arrived(part, g_c + k)
            pending.append(send(part, part, g_cf + k, sib))
        other = 1 - c
        arrived(ext.at[it, pl.ds(HW + OWN * (2 * y + other), OWN)], g_p)
        for k in (1, 3, 2):
            arrived(ext.at[it, pl.ds(HW + OWN * (2 * wrap(y - k, NY) + other), OWN)], g_pf + k)
        arrived(ext.at[it, pl.ds(OWN * other, OWN)], g_h + 2)
        arrived(ext.at[it, pl.ds(HW + PB + OWN * other, OWN)], g_h + 3)
        arrived(ext.at[it, pl.ds(EXT, HUBS), pl.ds(8 * (2 * y + other), 8)], g_c)
        for k in (1, 3, 2):
            arrived(ext.at[it, pl.ds(EXT, HUBS), pl.ds(8 * (2 * wrap(y - k, NY) + other), 8)], g_cf + k)

        def products(g, total):
            for u in range(8):
                t = 8 * g + u
                high, low = split(ext[it, idx[NT + t]])
                left = jnp.concatenate(
                    [jnp.concatenate([high, high], axis=1), jnp.concatenate([low, jnp.zeros_like(low)], axis=1)], axis=0
                )
                both = jnp.dot(left, weights[idx[t]], preferred_element_type=F32)
                total = total * flt[t] + (both[:K] + both[K:])
                prods[t] = total
            return total

        lax.fori_loop(0, NT // 8, products, jnp.zeros((K, TB), F32))

        def partial(r):
            return prods[idx[2 * NT + r]] * flt[NT + r]

        g_s = sems(NY)
        for k in (1, 3, 2, 0):
            for j in range(OWN):
                ssend[k, j] = partial(OWN * (2 * wrap(y + k, NY) + other) + j)
            pending.append(send(ssend.at[k], srecv.at[it, k], g_s + k, sib))
        g_r = sems(NY)
        for k in (1, 3, 2):
            arrived(srecv.at[it, k], g_s + k)
            for j in range(OWN):
                rsum[k, j] = partial(OWN * (2 * wrap(y + k, NY) + c) + j) + srecv[it, k, j]
            pending.append(send(rsum.at[k], rrecv.at[it, k], g_r + k, at_y(k)))
        arrived(srecv.at[it, 0], g_s)
        for k in (1, 3, 2):
            arrived(rrecv.at[it, k], g_r + k)
        for j in range(OWN):
            summed = partial(OWN * q + j) + srecv[it, 0, j]
            for k in (1, 3, 2):
                summed = summed + rrecv[it, k, j]
            image[:, TB * j : TB * (j + 1)] = state[0:K, TB * j : TB * (j + 1)] - summed

        held = state[...]
        w = image[...]
        g0 = nt(held, held)
        pay[it, :, 0:128] = g0[:K]
        pay[it, :, 128:256] = g0[K:]
        pay[it, :, 256:384] = nt(w, held)
        pay[it, :, 384:512] = jnp.concatenate([nt(w, w), jnp.zeros((K, K), F32)], axis=1)
        g_a = sems()
        for k in range(1, N_COL):
            peer = wrap(q + k, N_COL)
            send(pay.at[it, pl.ds(8 * peer, 8)], ra.at[it, q], g_a, (d, peer))
        pending.append((ra.at[it, pl.ds(0, N_COL - 1)], g_a))
        ra[it, q] = pay[it, pl.ds(8 * q, 8)]
        arrived(ra.at[it, pl.ds(0, N_COL - 1)], g_a)
        total = ra[it, 0]
        for k in range(1, N_COL):
            total = total + ra[it, k]
        rb1[it, z] = total
        g_b = sems()
        for k in range(1, NZ):
            send(rb1.at[it, z], rb1.at[it, z], g_b, at_xz(0, k))
        pending.append((rb1.at[it, pl.ds(0, NZ - 1)], g_b))
        arrived(rb1.at[it, pl.ds(0, NZ - 1)], g_b)
        total = rb1[it, 0]
        for k in range(1, NZ):
            total = total + rb1[it, k]
        rb2[it, x] = total
        g_b2 = sems()
        for i in range(1, NX):
            send(rb2.at[it, x], rb2.at[it, x], g_b2, at_xz(i, 0))
        pending.append((rb2.at[it, pl.ds(0, NX - 1)], g_b2))
        arrived(rb2.at[it, pl.ds(0, NX - 1)], g_b2)
        total = rb2[it, 0]
        for k in range(1, NX):
            total = total + rb2[it, k]
        rcbuf[it, q] = total
        g_d = sems()
        for k in range(1, N_COL):
            send(rcbuf.at[it, q], rcbuf.at[it, q], g_d, (d, wrap(q + k, N_COL)))
        pending.append((rcbuf.at[it, pl.ds(0, N_COL - 1)], g_d))
        arrived(rcbuf.at[it, pl.ds(0, N_COL - 1)], g_d)
        moments = jnp.concatenate([rcbuf[it, k] for k in range(N_COL)], axis=0)
        gvd = jnp.concatenate([moments[:, 0:128], moments[:, 128:256]], axis=0)
        cross = moments[:, 256:384]
        ww = moments[:, 384 : 384 + K]
        ritz_t = cross[:, 0:K]
        ritz_out[...] = ritz_t.T

        coeff = rot[it]
        c1, c2, c3 = coeff[:, 0:K], coeff[:, K : 2 * K], coeff[:, 2 * K :]
        shift = nn(c2, ritz_t)
        yvd = jnp.concatenate([c1 - shift, c3], axis=1)
        zvd = jnp.concatenate([-shift, c3], axis=1)
        lower = jnp.concatenate([cross, ww], axis=1)
        yall = jnp.concatenate([yvd, c2], axis=1)
        kall = jnp.concatenate([nn(yall, jnp.concatenate([gvd, cross], axis=0)), nt(yall, lower)], axis=1)
        reduced = nt(kall, yall)
        inverse = eliminate(0.5 * (reduced + reduced.T))
        zall = jnp.concatenate([zvd, c2], axis=1)
        mix = jnp.concatenate([nn(inverse, yall), nn(inverse, zall)], axis=0)
        state[...] = nn(mix, jnp.concatenate([held, w], axis=0))

        for item in pending:
            if isinstance(item, tuple):
                sent(*item)
            else:
                item.wait_send()
        return carry

    lax.fori_loop(0, ITERS, step, 0)
    vec_out[...] = state[0:K]
    dir_out[...] = state[K:]


def plan(band_rows, band_cols, hub_rows, hub_slots, hub_blocks):
    rows = jnp.concatenate([band_rows, hub_rows])
    cols = jnp.concatenate([band_cols, EXT + hub_slots])
    at = jnp.arange(NT, dtype=jnp.int32)
    before = (rows[None, :] < rows[:, None]) | ((rows[None, :] == rows[:, None]) & (at[None, :] < at[:, None]))
    place = jnp.sum(before.astype(jnp.int32), axis=1)
    chosen = (place[None, :] == at[:, None]).astype(jnp.int32)
    order = jnp.sum(chosen * at[None, :], axis=1)
    ordered_cols = jnp.sum(chosen * cols[None, :], axis=1)
    ordered_rows = jnp.sum(chosen * rows[None, :], axis=1)
    keep = (ordered_rows == jnp.roll(ordered_rows, 1)) & (at > 0)
    upto = jnp.sum((rows[None, :] <= at[:, None]).astype(jnp.int32), axis=1)
    has = jnp.any(rows[None, :] == at[:, None], axis=1)
    last = jnp.maximum(upto - 1, 0)
    d, q = lax.axis_index("dom"), lax.axis_index("col")
    hub = hub_blocks[d] - d * PB - q * OWN == jnp.arange(OWN, dtype=jnp.int32)
    return jnp.concatenate([order, ordered_cols, last]), jnp.concatenate([keep, has, hub]).astype(F32)


def per_device(
    band_tiles, band_rows, band_cols, hub_tiles, hub_rows, hub_slots, hub_blocks,
    start_vectors, prior_directions, rotation,
):
    idx, flt = plan(band_rows, band_cols, hub_rows, hub_slots, hub_blocks)
    smem = pl.BlockSpec(memory_space=pltpu.SMEM)
    vmem = pl.BlockSpec(memory_space=pltpu.VMEM)
    anywhere = pl.BlockSpec(memory_space=pl.ANY)
    rows = K * 0 + 512
    vec, direc, ritz = pl.pallas_call(
        kernel,
        out_shape=(
            jax.ShapeDtypeStruct((K, rows), F32),
            jax.ShapeDtypeStruct((K, rows), F32),
            jax.ShapeDtypeStruct((K, K), F32),
        ),
        in_specs=[smem, smem, vmem, vmem, vmem, anywhere, anywhere],
        out_specs=(vmem, vmem, vmem),
        scratch_shapes=[
            pltpu.VMEM((NT, TB, TB), F32),
            pltpu.VMEM((NT, 2 * TB, TB), BF16),
            pltpu.VMEM((2 * K, rows), F32),
            pltpu.VMEM((K, rows), F32),
            pltpu.VMEM((ITERS, OWN, K, TB), F32),
            pltpu.VMEM((ITERS, EXT + HUBS, K, TB), F32),
            pltpu.VMEM((ITERS, K, TB), F32),
            pltpu.VMEM((ITERS, N_COL, 8, TB), F32),
            pltpu.VMEM((ITERS, N_DOM, 8, TB), F32),
            pltpu.VMEM((NT, K, TB), F32),
            pltpu.VMEM((NY, OWN, K, TB), F32),
            pltpu.VMEM((ITERS, NY, OWN, K, TB), F32),
            pltpu.VMEM((NY, OWN, K, TB), F32),
            pltpu.VMEM((ITERS, NY, OWN, K, TB), F32),
            pltpu.VMEM((ITERS, K, 512), F32),
            pltpu.VMEM((ITERS, N_COL, 8, 512), F32),
            pltpu.VMEM((ITERS, NZ, 8, 512), F32),
            pltpu.VMEM((ITERS, NX, 8, 512), F32),
            pltpu.VMEM((ITERS, N_COL, 8, 512), F32),
            pltpu.VMEM((8, 512), F32),
            pltpu.SemaphoreType.DMA((2,)),
            pltpu.SemaphoreType.DMA((ITERS, 40)),
            pltpu.SemaphoreType.DMA((ITERS, 40)),
        ],
        compiler_params=pltpu.CompilerParams(
            collective_id=0, has_side_effects=True, vmem_limit_bytes=48 * 1024 * 1024
        ),
        name="lobpcg",
    )(
        idx, flt, start_vectors.T, prior_directions.T, jnp.transpose(rotation, (0, 2, 1)),
        band_tiles, hub_tiles,
    )
    return vec.T, direc.T, ritz


def solution(mesh):
    return jax.shard_map(
        per_device,
        mesh=mesh,
        in_specs=(
            P(("dom", "col"), None, None),
            P(("dom", "col")),
            P(("dom", "col")),
            P(("dom", "col"), None, None),
            P(("dom", "col")),
            P(("dom", "col")),
            P(),
            P(("dom", "col"), None),
            P(("dom", "col"), None),
            P(),
        ),
        out_specs=(P(("dom", "col"), None), P(("dom", "col"), None), P()),
        check_vma=False,
    )
```

```python
import jax
import jax.numpy as jnp
from jax import lax
from jax.experimental import pallas as pl
from jax.experimental.pallas import tpu as pltpu
from jax.sharding import PartitionSpec as P

TB = 128
K = 64
PB = 32
ITERS = 2
HW = 8
NZ = 8
NX = 4
NY = 4
N_DOM = 32
N_COL = 8
TPD = 24
HTD = 8
NT = TPD + HTD
OWN = 4
EXT = PB + 2 * HW
HUBS = 32
MESH = pl.DeviceIdType.MESH
F32 = jnp.float32
BF16 = jnp.bfloat16
HI = lax.Precision.HIGHEST


def wrap(value, count):
    return lax.rem(value + count, count)


def nn(a, b):
    return jnp.dot(a, b, precision=HI, preferred_element_type=F32)


def nt(a, b):
    return lax.dot_general(a, b, (((1,), (1,)), ((), ())), precision=HI, preferred_element_type=F32)


def split(value):
    high = value.astype(BF16)
    return high, (value - high.astype(F32)).astype(BF16)


def eliminate(matrix):
    full = (8, 2 * K)
    rows = lax.broadcasted_iota(jnp.int32, full, 0)
    lanes = lax.broadcasted_iota(jnp.int32, full, 1)
    wide = jnp.concatenate([matrix, jnp.zeros((K, K), F32)], axis=1)
    blocks = [jnp.where(lanes - K == rows + 8 * b, 1.0, wide[8 * b : 8 * b + 8]) for b in range(K // 8)]
    for home in range(K // 8):
        cols = [
            [jnp.broadcast_to(blocks[b][:, 8 * home + c : 8 * home + c + 1], full) for c in range(8)]
            for b in range(home, K // 8)
        ]
        work = [jnp.broadcast_to(blocks[home][r : r + 1, :], full) for r in range(8)]
        a = [[jnp.broadcast_to(cols[0][c][r : r + 1, :], full) for c in range(r + 1)] for r in range(8)]
        scale, done = [], []
        for c in range(8):
            scale.append(lax.rsqrt(a[c][c]))
            done.append(work[c] * scale[c])
            for r in range(c + 1, 8):
                a[r][c] = a[r][c] * scale[c]
            for r in range(c + 1, 8):
                for e in range(c + 1, r + 1):
                    a[r][e] = a[r][e] - a[r][c] * a[e][c]
                work[r] = work[r] - a[r][c] * done[c]
        back = [None] * 8
        for c in reversed(range(8)):
            value = done[c]
            for r in range(c + 1, 8):
                value = value - a[r][c] * back[r]
            back[c] = value * scale[c]
        for b in range(home + 1, K // 8):
            for c in range(8):
                blocks[b] = blocks[b] - cols[b - home][c] * back[c]
        for r in range(8):
            blocks[home] = jnp.where(rows == r, done[r], blocks[home])
    return jnp.concatenate(blocks, axis=0)[:, K:]


def plan(band_rows, band_cols, hub_rows, hub_slots):
    full = (NT, TB)
    sub = lax.broadcasted_iota(jnp.int32, full, 0)
    lane = lax.broadcasted_iota(jnp.int32, full, 1)
    key_s = jnp.zeros(full, jnp.int32)
    key_l = jnp.full(full, 4 * PB, jnp.int32)
    src_l = jnp.zeros(full, jnp.int32)
    for t in range(NT):
        key = band_rows[t] if t < TPD else PB + hub_rows[t - TPD]
        src = band_cols[t] if t < TPD else hub_slots[t - TPD]
        key_s = jnp.where(sub == t, key, key_s)
        key_l = jnp.where(lane == t, key, key_l)
        src_l = jnp.where(lane == t, src, src_l)

    def one(cond):
        return jnp.where(cond, 1, 0)

    same = jnp.where(sub < lane, one(key_s == key_l), 0)
    place = jnp.sum(one(key_s < key_l) + same, axis=0, keepdims=True)
    again = jnp.sum(same, axis=0, keepdims=True)
    place = jnp.where(lane < NT, jnp.broadcast_to(place, full), NT)
    chosen = one(place == sub)

    def across(value):
        return jnp.sum(value, axis=1, keepdims=True)

    columns = [
        across(chosen * lane),
        across(chosen * src_l),
        across(chosen * one(jnp.broadcast_to(again, full) > 0)),
        jnp.maximum(across(one(key_l <= sub)) - 1, 0),
        one(across(one(key_l == sub)) > 0),
        jnp.maximum(across(one(key_l <= sub + PB)) - 1, 0),
        one(across(one(key_l == sub + PB)) > 0),
    ]
    table = jnp.zeros(full, jnp.int32)
    for n, column in enumerate(columns):
        table = jnp.where(lane == n, jnp.broadcast_to(column, full), table)
    return table


def kernel(
    band_rows, band_cols, hub_rows, hub_slots, hub_blocks, vec_hbm, dir_hbm, rot_hbm, band_hbm, hub_hbm,
    vec_out, dir_out, ritz_out,
    tiles, weights, table_v, table, rot, xt, xt2,
    own, cand, hca, hubx, eb0, eb1, eb2, eh0, eh1, eh2, pr0, pr1, pr2,
    ssend, srecv, rsum, rrecv, pay, ra, rb1, rb2, rc, lsem, ssem, rsem,
):
    d = lax.axis_index("dom")
    q = lax.axis_index("col")
    x, z = d // NZ, d % NZ
    y, c = q // 2, q % 2
    other = 1 - c
    sib = (d, q + 1 - 2 * c)
    band, hub, prods = (eb0, eb1, eb2), (eh0, eh1, eh2), (pr0, pr1, pr2)

    def at_y(k):
        return (d, 2 * wrap(y + k, NY) + c)

    def at_xz(i, k):
        return (wrap(x + i, NX) * NZ + wrap(z + k, NZ), q)

    others = [(i, k) for i in range(NX) for k in range(NZ) if (i, k) != (0, 0)]
    partners = [(d, wrap(q + k, N_COL)) for k in range(1, N_COL)] + [at_xz(i, k) for i, k in others]

    local = []
    for n, (src, dst) in enumerate(
        (
            (vec_hbm, xt.at[pl.ds(0, K)]),
            (dir_hbm, xt.at[pl.ds(K, K)]),
            (band_hbm, tiles.at[pl.ds(0, TPD)]),
            (hub_hbm, tiles.at[pl.ds(TPD, HTD)]),
            (rot_hbm, rot),
        )
    ):
        local.append(pltpu.make_async_copy(src, dst, lsem.at[n]))
        local[n].start()
    barrier = pltpu.get_barrier_semaphore()
    for partner in partners:
        pl.semaphore_signal(barrier, inc=1, device_id=partner, device_id_type=MESH)

    counter = [0]
    pending = []

    def sems(n=1):
        counter[0] += n
        return counter[0] - n

    def send(src, dst, sem, device):
        copy = pltpu.make_async_remote_copy(
            src_ref=src, dst_ref=dst, send_sem=ssem.at[sem], recv_sem=rsem.at[sem],
            device_id=device, device_id_type=MESH,
        )
        copy.start()
        return copy

    def arrived(ref, sem):
        pltpu.make_async_copy(ref, ref, rsem.at[sem]).wait()

    def block_of(col):
        return pl.ds(HW + OWN * col, OWN)

    mask = [jnp.where(hub_blocks[d] - d * PB - q * OWN == j, 1.0, 0.0) for j in range(OWN)]
    names = ("ha", "p", "hb", "pf", "h", "hc", "hcf")
    gsem = [dict(zip(names, [sems(n) for n in (1, NY, 1, NY, 4, NY, NY)])) for _ in range(3)]

    def g_start(g, ref, first):
        pick = jnp.zeros((K, TB), F32)
        for j in range(OWN):
            block = ref[first : first + K, TB * j : TB * (j + 1)]
            own[g, j] = block
            band[g][HW + OWN * q + j] = block
            pick = pick + block * mask[j]
        cand[g] = pick
        for k in range(1, N_COL):
            peer = wrap(q + k, N_COL)
            send(cand.at[g, pl.ds(8 * peer, 8)], hca.at[g, q], gsem[g]["ha"], (d, peer))
        pending.append((hca.at[g, pl.ds(0, N_COL - 1)], gsem[g]["ha"]))
        hca[g, q] = cand[g, pl.ds(8 * q, 8)]
        mine = band[g].at[block_of(q)]
        for k in (2, 1, 3):
            pending.append(send(own.at[g], mine, gsem[g]["p"] + k, at_y(k)))
        pending.append(send(own.at[g], mine, gsem[g]["p"], sib))

    def g_hub(g):
        arrived(hca.at[g, pl.ds(0, N_COL - 1)], gsem[g]["ha"])
        piece = hca[g, 0]
        for k in range(1, N_COL):
            piece = piece + hca[g, k]
        hubx[g, d] = piece
        for i, k in sorted(others, key=lambda p: -min(p[0], NX - p[0]) - min(p[1], NZ - p[1])):
            send(hubx.at[g, d], hubx.at[g, d], gsem[g]["hb"], at_xz(i, k))
        pending.append((hubx.at[g, pl.ds(0, N_DOM - 1)], gsem[g]["hb"]))

    def g_panel(g):
        for k in (1, 3, 2):
            block = band[g].at[block_of(2 * wrap(y - k, NY) + c)]
            arrived(block, gsem[g]["p"] + k)
            pending.append(send(block, block, gsem[g]["pf"] + k, sib))
        low, high = band[g].at[pl.ds(OWN * c, OWN)], band[g].at[pl.ds(HW + PB + OWN * c, OWN)]
        pending.append(send(band[g].at[block_of(N_COL - 2 + c)], low, gsem[g]["h"], (wrap(d + 1, N_DOM), q)))
        pending.append(send(band[g].at[block_of(c)], high, gsem[g]["h"] + 1, (wrap(d - 1, N_DOM), q)))

    def g_spread(g):
        arrived(hubx.at[g, pl.ds(0, N_DOM - 1)], gsem[g]["hb"])
        mine = hub[g].at[pl.ds(0, HUBS), pl.ds(8 * q, 8)]
        for k in (2, 1, 3):
            pending.append(send(hubx.at[g], mine, gsem[g]["hc"] + k, at_y(k)))
        pending.append(send(hubx.at[g], mine, gsem[g]["hc"], sib))
        for s in range(HUBS):
            hub[g][s, pl.ds(8 * q, 8)] = hubx[g, s]

    def g_halo(g):
        for n, at in enumerate((OWN * c, HW + PB + OWN * c)):
            part = band[g].at[pl.ds(at, OWN)]
            arrived(part, gsem[g]["h"] + n)
            pending.append(send(part, part, gsem[g]["h"] + 2 + n, sib))

    def g_band_end(g):
        arrived(band[g].at[block_of(2 * y + other)], gsem[g]["p"])
        for k in (1, 3, 2):
            arrived(band[g].at[block_of(2 * wrap(y - k, NY) + other)], gsem[g]["pf"] + k)
        arrived(band[g].at[pl.ds(OWN * other, OWN)], gsem[g]["h"] + 2)
        arrived(band[g].at[pl.ds(HW + PB + OWN * other, OWN)], gsem[g]["h"] + 3)

    def g_pass(g):
        for k in (1, 3, 2):
            part = hub[g].at[pl.ds(0, HUBS), pl.ds(8 * (2 * wrap(y - k, NY) + c), 8)]
            arrived(part, gsem[g]["hc"] + k)
            pending.append(send(part, part, gsem[g]["hcf"] + k, sib))

    def g_hub_end(g):
        arrived(hub[g].at[pl.ds(0, HUBS), pl.ds(8 * (2 * y + other), 8)], gsem[g]["hc"])
        for k in (1, 3, 2):
            part = hub[g].at[pl.ds(0, HUBS), pl.ds(8 * (2 * wrap(y - k, NY) + other), 8)]
            arrived(part, gsem[g]["hcf"] + k)

    def multiply(g, source, first, count):
        def group(n, total):
            for u in range(8):
                t = first + 8 * n + u
                high, low = split(source[table[t, 1]])
                left = jnp.concatenate(
                    [jnp.concatenate([high, high], axis=1), jnp.concatenate([low, jnp.zeros_like(low)], axis=1)], axis=0
                )
                both = jnp.dot(left, weights[table[t, 0]], preferred_element_type=F32)
                total = total * table[t, 2].astype(F32) + (both[:K] + both[K:])
                prods[g][t] = total
            return total

        lax.fori_loop(0, count // 8, group, jnp.zeros((K, TB), F32))

    def row_sum(g, r):
        return prods[g][table[r, 3]] * table[r, 4].astype(F32) + prods[g][table[r, 5]] * table[r, 6].astype(F32)

    ssems = [(sems(NY), sems(NY)) for _ in range(ITERS)]

    def scatter_start(n, rows_of):
        for k in (2, 1, 3, 0):
            for j, block in enumerate(rows_of(OWN * (2 * wrap(y + k, NY) + other))):
                ssend[n, k, j] = block
            pending.append(send(ssend.at[n, k], srecv.at[n, k], ssems[n][0] + k, sib))
        for k in (2, 1, 3):
            blocks = rows_of(OWN * (2 * wrap(y + k, NY) + c))
            arrived(srecv.at[n, k], ssems[n][0] + k)
            for j, block in enumerate(blocks):
                rsum[n, k, j] = block + srecv[n, k, j]
            pending.append(send(rsum.at[n, k], rrecv.at[n, k], ssems[n][1] + k, at_y(k)))

    def scatter_end(n, rows_of):
        blocks = rows_of(OWN * q)
        arrived(srecv.at[n, 0], ssems[n][0])
        blocks = [block + srecv[n, 0, j] for j, block in enumerate(blocks)]
        for k in (1, 3, 2):
            arrived(rrecv.at[n, k], ssems[n][1] + k)
            blocks = [block + rrecv[n, k, j] for j, block in enumerate(blocks)]
        return jnp.concatenate(blocks, axis=1)

    asems = [sems(4) for _ in range(ITERS + 1)]

    def a_start(n):
        for k in range(1, N_COL):
            peer = wrap(q + k, N_COL)
            send(pay.at[n, pl.ds(8 * peer, 8)], ra.at[n, q], asems[n], (d, peer))
        pending.append((ra.at[n, pl.ds(0, N_COL - 1)], asems[n]))
        ra[n, q] = pay[n, pl.ds(8 * q, 8)]

    def a_sum(ref, n, count, sem):
        arrived(ref.at[n, pl.ds(0, count - 1)], sem)
        total = ref[n, 0]
        for k in range(1, count):
            total = total + ref[n, k]
        return total

    def a_z(n):
        rb1[n, z] = a_sum(ra, n, N_COL, asems[n])
        for k in (4, 3, 5, 2, 6, 1, 7):
            send(rb1.at[n, z], rb1.at[n, z], asems[n] + 1, at_xz(0, k))
        pending.append((rb1.at[n, pl.ds(0, NZ - 1)], asems[n] + 1))

    def a_x(n):
        rb2[n, x] = a_sum(rb1, n, NZ, asems[n] + 1)
        for i in (2, 1, 3):
            send(rb2.at[n, x], rb2.at[n, x], asems[n] + 2, at_xz(i, 0))
        pending.append((rb2.at[n, pl.ds(0, NX - 1)], asems[n] + 2))

    def a_back(n):
        rc[n, q] = a_sum(rb2, n, NX, asems[n] + 2)
        for k in range(1, N_COL):
            send(rc.at[n, q], rc.at[n, q], asems[n] + 3, (d, wrap(q + k, N_COL)))
        pending.append((rc.at[n, pl.ds(0, N_COL - 1)], asems[n] + 3))

    def a_end(n):
        arrived(rc.at[n, pl.ds(0, N_COL - 1)], asems[n] + 3)
        return jnp.concatenate([rc[n, k] for k in range(N_COL)], axis=0)

    def moments(ref):
        return jnp.concatenate([nt(ref[2 * K :], ref[...]), jnp.zeros((K, K), F32)], axis=1)

    def coefficients(it, gvd, sums):
        lower = sums[:, : 3 * K]
        cross = sums[:, : 2 * K]
        ritz_t = sums[:, :K]
        coeff = rot[it]
        c1, c2, c3 = coeff[:, 0:K], coeff[:, K : 2 * K], coeff[:, 2 * K :]
        shift = nn(c2, ritz_t)
        yall = jnp.concatenate([c1 - shift, c3, c2], axis=1)
        zall = jnp.concatenate([-shift, c3, c2], axis=1)
        upper = jnp.concatenate([gvd, cross], axis=0)
        kall = jnp.concatenate([nn(yall, upper), nt(yall, lower)], axis=1)
        reduced = nt(kall, yall)
        inverse = eliminate(0.5 * (reduced + reduced.T))
        return jnp.concatenate([nn(inverse, yall), nn(inverse, zall)], axis=0), upper, lower

    local[0].wait()
    pl.semaphore_wait(barrier, len(partners))
    g_start(0, xt, 0)
    local[1].wait()
    both = xt[0 : 2 * K, :]
    gram = nt(both, both)
    pay[0] = jnp.concatenate([gram[:K], gram[K:]], axis=1)
    a_start(0)
    table_v[...] = plan(band_rows, band_cols, hub_rows, hub_slots)
    to_smem = pltpu.make_async_copy(table_v, table, lsem.at[5])
    to_smem.start()
    g_hub(0)
    for n in (2, 3, 4):
        local[n].wait()

    def prepare(t, carry):
        high, low = split(tiles[t].T)
        weights[t, 0:TB] = high
        weights[t, TB:] = low
        return carry

    lax.fori_loop(0, NT // 2, prepare, 0)
    a_z(0)
    lax.fori_loop(NT // 2, NT, prepare, 0)
    to_smem.wait()
    g_panel(0)
    g_spread(0)
    g_halo(0)
    g_band_end(0)
    multiply(0, band[0], 0, TPD)
    g_pass(0)
    g_start(1, xt, K)
    g_hub_end(0)
    multiply(0, hub[0], TPD, HTD)
    a_x(0)
    g_hub(1)

    def first_rows(r):
        return [row_sum(0, r + j) for j in range(OWN)]

    scatter_start(0, first_rows)
    a_back(0)
    g_panel(1)
    xt[2 * K :] = xt[0:K] - scatter_end(0, first_rows)
    pay[1] = moments(xt)
    a_start(1)
    g_start(2, xt, 2 * K)
    sums0 = a_end(0)
    gvd = jnp.concatenate([sums0[:, : 2 * K], sums0[:, 2 * K :]], axis=0)
    g_spread(1)
    g_halo(1)
    a_z(1)
    g_hub(2)
    g_band_end(1)
    multiply(1, band[1], 0, TPD)
    a_x(1)
    g_panel(2)
    g_pass(1)
    a_back(1)
    g_spread(2)
    g_halo(2)
    g_hub_end(1)
    multiply(1, hub[1], TPD, HTD)
    g_band_end(2)
    multiply(2, band[2], 0, TPD)
    sums1 = a_end(1)
    mix, upper, lower = coefficients(0, gvd, sums1)
    g_pass(2)
    mix_high, mix_low = split(mix[:K])
    mix_both = jnp.concatenate([mix_high, mix_low], axis=0)
    xt2[0 : 2 * K] = nn(mix, xt[...])
    carried = jnp.concatenate([nn(mix, upper), nt(mix, lower)], axis=1)
    gvd = nt(carried, mix)
    g_hub_end(2)
    multiply(2, hub[2], TPD, HTD)

    def second_rows(r):
        stack = jnp.concatenate(
            [jnp.concatenate([row_sum(g, r + j) for j in range(OWN)], axis=1) for g in range(3)], axis=0
        )
        high, low = split(stack)
        one = jnp.dot(mix_both, high, preferred_element_type=F32)
        two = jnp.dot(mix_high, low, preferred_element_type=F32)
        out = one[:K] + one[K:] + two
        return [out[:, TB * j : TB * (j + 1)] for j in range(OWN)]

    scatter_start(1, second_rows)
    xt2[2 * K :] = xt2[0:K] - scatter_end(1, second_rows)
    pay[2] = moments(xt2)
    a_start(2)
    a_z(2)
    a_x(2)
    a_back(2)
    sums2 = a_end(2)
    ritz_out[...] = sums2[:, :K].T
    mix2, _, _ = coefficients(1, gvd, sums2)
    final = nn(mix2, xt2[...])
    vec_out[...] = final[:K]
    dir_out[...] = final[K:]

    for item in pending:
        if isinstance(item, tuple):
            ref, sem = item
            pltpu.make_async_copy(ref, ref, ssem.at[sem]).wait()
        else:
            item.wait_send()


def per_device(
    band_tiles, band_rows, band_cols, hub_tiles, hub_rows, hub_slots, hub_blocks,
    start_vectors, prior_directions, rotation,
):
    smem = pl.BlockSpec(memory_space=pltpu.SMEM)
    vmem = pl.BlockSpec(memory_space=pltpu.VMEM)
    hbm = pl.BlockSpec(memory_space=pltpu.HBM)
    rows = start_vectors.shape[0]
    ext = [pltpu.VMEM((EXT, K, TB), F32)] * 3 + [pltpu.VMEM((HUBS, K, TB), F32)] * 3
    vec, direc, ritz = pl.pallas_call(
        kernel,
        out_shape=(
            jax.ShapeDtypeStruct((K, rows), F32),
            jax.ShapeDtypeStruct((K, rows), F32),
            jax.ShapeDtypeStruct((K, K), F32),
        ),
        in_specs=[smem] * 5 + [hbm] * 5,
        out_specs=(vmem, vmem, vmem),
        scratch_shapes=[
            pltpu.VMEM((NT, TB, TB), F32),
            pltpu.VMEM((NT, 2 * TB, TB), BF16),
            pltpu.VMEM((NT, TB), jnp.int32),
            pltpu.SMEM((NT, TB), jnp.int32),
            pltpu.VMEM((ITERS, K, 3 * K), F32),
            pltpu.VMEM((3 * K, rows), F32),
            pltpu.VMEM((3 * K, rows), F32),
            pltpu.VMEM((3, OWN, K, TB), F32),
            pltpu.VMEM((3, K, TB), F32),
            pltpu.VMEM((3, N_COL, 8, TB), F32),
            pltpu.VMEM((3, N_DOM, 8, TB), F32),
            *ext,
            *[pltpu.VMEM((NT, K, TB), F32)] * 3,
            pltpu.VMEM((ITERS, NY, OWN, K, TB), F32),
            pltpu.VMEM((ITERS, NY, OWN, K, TB), F32),
            pltpu.VMEM((ITERS, NY, OWN, K, TB), F32),
            pltpu.VMEM((ITERS, NY, OWN, K, TB), F32),
            pltpu.VMEM((ITERS + 1, K, 4 * K), F32),
            pltpu.VMEM((ITERS + 1, N_COL, 8, 4 * K), F32),
            pltpu.VMEM((ITERS + 1, NZ, 8, 4 * K), F32),
            pltpu.VMEM((ITERS + 1, NX, 8, 4 * K), F32),
            pltpu.VMEM((ITERS + 1, N_COL, 8, 4 * K), F32),
            pltpu.SemaphoreType.DMA((6,)),
            pltpu.SemaphoreType.DMA((100,)),
            pltpu.SemaphoreType.DMA((100,)),
        ],
        compiler_params=pltpu.CompilerParams(
            collective_id=0, has_side_effects=True, vmem_limit_bytes=56 * 1024 * 1024
        ),
        name="lobpcg",
    )(
        band_rows, band_cols, hub_rows, hub_slots, hub_blocks, start_vectors.T, prior_directions.T,
        jnp.transpose(rotation, (0, 2, 1)), band_tiles, hub_tiles,
    )
    return vec.T, direc.T, ritz


def solution(mesh):
    return jax.shard_map(
        per_device,
        mesh=mesh,
        in_specs=(
            P(("dom", "col"), None, None),
            P(("dom", "col")),
            P(("dom", "col")),
            P(("dom", "col"), None, None),
            P(("dom", "col")),
            P(("dom", "col")),
            P(),
            P(("dom", "col"), None),
            P(("dom", "col"), None),
            P(),
        ),
        out_specs=(P(("dom", "col"), None), P(("dom", "col"), None), P()),
        check_vma=False,
    )
```

```python
import jax
import jax.numpy as jnp
from jax import lax
from jax.experimental import pallas as pl
from jax.experimental.pallas import tpu as pltpu
from jax.sharding import PartitionSpec as P

TB = 128
K = 64
PB = 32
ITERS = 2
HW = 8
NZ = 8
NX = 4
NY = 4
N_DOM = 32
N_COL = 8
TPD = 24
HTD = 8
NT = TPD + HTD
OWN = 4
EXT = PB + 2 * HW
HUBS = 32
HALF = 32
MESH = pl.DeviceIdType.MESH
F32 = jnp.float32
BF16 = jnp.bfloat16
HI = lax.Precision.HIGHEST


def wrap(value, count):
    return lax.rem(value + count, count)


def nn(a, b):
    return jnp.dot(a, b, precision=HI, preferred_element_type=F32)


def nt(a, b):
    return lax.dot_general(a, b, (((1,), (1,)), ((), ())), precision=HI, preferred_element_type=F32)


def split(value):
    high = value.astype(BF16)
    return high, (value - high.astype(F32)).astype(BF16)


def eliminate(matrix):
    full = (8, 2 * K)
    rows = lax.broadcasted_iota(jnp.int32, full, 0)
    lanes = lax.broadcasted_iota(jnp.int32, full, 1)
    wide = jnp.concatenate([matrix, jnp.zeros((K, K), F32)], axis=1)
    blocks = [jnp.where(lanes - K == rows + 8 * b, 1.0, wide[8 * b : 8 * b + 8]) for b in range(K // 8)]
    for home in range(K // 8):
        cols = [
            [jnp.broadcast_to(blocks[b][:, 8 * home + c : 8 * home + c + 1], full) for c in range(8)]
            for b in range(home, K // 8)
        ]
        work = [jnp.broadcast_to(blocks[home][r : r + 1, :], full) for r in range(8)]
        a = [[jnp.broadcast_to(cols[0][c][r : r + 1, :], full) for c in range(r + 1)] for r in range(8)]
        scale, done = [], []
        for c in range(8):
            scale.append(lax.rsqrt(a[c][c]))
            done.append(work[c] * scale[c])
            for r in range(c + 1, 8):
                a[r][c] = a[r][c] * scale[c]
            for r in range(c + 1, 8):
                for e in range(c + 1, r + 1):
                    a[r][e] = a[r][e] - a[r][c] * a[e][c]
                work[r] = work[r] - a[r][c] * done[c]
        back = [None] * 8
        for c in reversed(range(8)):
            value = done[c]
            for r in range(c + 1, 8):
                value = value - a[r][c] * back[r]
            back[c] = value * scale[c]
        for b in range(home + 1, K // 8):
            for c in range(8):
                blocks[b] = blocks[b] - cols[b - home][c] * back[c]
        for r in range(8):
            blocks[home] = jnp.where(rows == r, done[r], blocks[home])
    return jnp.concatenate(blocks, axis=0)[:, K:]


def plan(band_rows, band_cols, hub_rows, hub_slots):
    full = (NT, TB)
    sub = lax.broadcasted_iota(jnp.int32, full, 0)
    lane = lax.broadcasted_iota(jnp.int32, full, 1)
    key_s = jnp.zeros(full, jnp.int32)
    key_l = jnp.full(full, 4 * PB, jnp.int32)
    src_l = jnp.zeros(full, jnp.int32)
    for t in range(NT):
        key = band_rows[t] if t < TPD else PB + hub_rows[t - TPD]
        src = band_cols[t] if t < TPD else hub_slots[t - TPD]
        key_s = jnp.where(sub == t, key, key_s)
        key_l = jnp.where(lane == t, key, key_l)
        src_l = jnp.where(lane == t, src, src_l)

    def one(cond):
        return jnp.where(cond, 1, 0)

    same = jnp.where(sub < lane, one(key_s == key_l), 0)
    place = jnp.sum(one(key_s < key_l) + same, axis=0, keepdims=True)
    again = jnp.sum(same, axis=0, keepdims=True)
    place = jnp.where(lane < NT, jnp.broadcast_to(place, full), NT)
    chosen = one(place == sub)

    def across(value):
        return jnp.sum(value, axis=1, keepdims=True)

    columns = [
        across(chosen * lane),
        across(chosen * src_l),
        across(chosen * one(jnp.broadcast_to(again, full) > 0)),
        jnp.maximum(across(one(key_l <= sub)) - 1, 0),
        one(across(one(key_l == sub)) > 0),
        jnp.maximum(across(one(key_l <= sub + PB)) - 1, 0),
        one(across(one(key_l == sub + PB)) > 0),
    ]
    table = jnp.zeros(full, jnp.int32)
    for n, column in enumerate(columns):
        table = jnp.where(lane == n, jnp.broadcast_to(column, full), table)
    return table


def kernel(
    band_rows, band_cols, hub_rows, hub_slots, hub_blocks, vec_hbm, dir_hbm, rot_hbm, band_hbm, hub_hbm,
    mix_out, xt2, ritz_out,
    tiles, weights, table_v, table, rot, xt,
    own, cand, hca, hubz, eb0, eb1, eb2, eh0, eh1, eh2, pr0, pr1, pr2, mixed,
    ssend, srecv, rsum, rrecv, pay0, ra0, rb0, rx0, rc0, pay1, ra1, rb1, rx1, rc1,
    wpay, wrecv, wplane, wz, wend, lsem, ssem, rsem,
):
    d = lax.axis_index("dom")
    q = lax.axis_index("col")
    x, z = d // NZ, d % NZ
    y, c = q // 2, q % 2
    other = 1 - c
    sib = (d, q + 1 - 2 * c)
    band, hub, prods = (eb0, eb1, eb2), (eh0, eh1, eh2), (pr0, pr1, pr2)

    def at_y(k):
        return (d, 2 * wrap(y + k, NY) + c)

    def at_xz(i, k):
        return (wrap(x + i, NX) * NZ + wrap(z + k, NZ), q)

    others = [(i, k) for i in range(NX) for k in range(NZ) if (i, k) != (0, 0)]
    partners = [(d, wrap(q + k, N_COL)) for k in range(1, N_COL)] + [at_xz(i, k) for i, k in others]

    local = []
    for n, (src, dst) in enumerate(
        (
            (vec_hbm, xt.at[pl.ds(0, K)]),
            (dir_hbm, xt.at[pl.ds(K, K)]),
            (band_hbm, tiles.at[pl.ds(0, TPD)]),
            (hub_hbm, tiles.at[pl.ds(TPD, HTD)]),
            (rot_hbm, rot),
        )
    ):
        local.append(pltpu.make_async_copy(src, dst, lsem.at[n]))
        local[n].start()
    barrier = pltpu.get_barrier_semaphore()
    for partner in partners:
        pl.semaphore_signal(barrier, inc=1, device_id=partner, device_id_type=MESH)

    counter = [0]
    pending = []

    def sems(n=1):
        counter[0] += n
        return counter[0] - n

    def send(src, dst, sem, device):
        copy = pltpu.make_async_remote_copy(
            src_ref=src, dst_ref=dst, send_sem=ssem.at[sem], recv_sem=rsem.at[sem],
            device_id=device, device_id_type=MESH,
        )
        copy.start()
        return copy

    def arrived(ref, sem):
        pltpu.make_async_copy(ref, ref, rsem.at[sem]).wait()

    def block_of(col):
        return pl.ds(HW + OWN * col, OWN)

    mask = [jnp.where(hub_blocks[d] - d * PB - q * OWN == j, 1.0, 0.0) for j in range(OWN)]
    names = ("ha", "p", "hb", "pf", "h", "hc", "hcf")
    gsem = [dict(zip(names, [sems(n) for n in (1, NY, 1, NY, 4, NX, NX)])) for _ in range(3)]
    hub_row = jnp.clip(hub_blocks[d] - d * PB, 0, PB - 1)

    def g_start(g, ref, first):
        for j in range(OWN):
            block = ref[first : first + K, TB * j : TB * (j + 1)]
            own[g, j] = block
            band[g][HW + OWN * q + j] = block
        mine = band[g].at[block_of(q)]
        for k in (2, 1, 3):
            pending.append(send(own.at[g], mine, gsem[g]["p"] + k, at_y(k)))
        pending.append(send(own.at[g], mine, gsem[g]["p"], sib))

    def masked(ref, first):
        pick = jnp.zeros((K, TB), F32)
        for j in range(OWN):
            pick = pick + ref[first : first + K, TB * j : TB * (j + 1)] * mask[j]
        return pick

    def g_hub_start(g, term):
        cand[g] = term
        for k in range(1, N_COL):
            peer = wrap(q + k, N_COL)
            send(cand.at[g, pl.ds(HALF * (peer % 2), HALF)], hca.at[g, q], gsem[g]["ha"], (d, peer))
        pending.append((hca.at[g, pl.ds(0, N_COL - 1)], gsem[g]["ha"]))
        hca[g, q] = cand[g, pl.ds(HALF * c, HALF)]

    def g_hub(g, base=None):
        arrived(hca.at[g, pl.ds(0, N_COL - 1)], gsem[g]["ha"])
        piece = hca[g, 0]
        for k in range(1, N_COL):
            piece = piece + hca[g, k]
        hubz[g, z] = piece if base is None else base - piece
        for k in (4, 3, 5, 2, 6, 1, 7):
            send(hubz.at[g, z], hubz.at[g, z], gsem[g]["hb"], at_xz(0, k))
        pending.append((hubz.at[g, pl.ds(0, NZ - 1)], gsem[g]["hb"]))

    def g_panel(g):
        for k in (1, 3, 2):
            block = band[g].at[block_of(2 * wrap(y - k, NY) + c)]
            arrived(block, gsem[g]["p"] + k)
            pending.append(send(block, block, gsem[g]["pf"] + k, sib))
        low, high = band[g].at[pl.ds(OWN * c, OWN)], band[g].at[pl.ds(HW + PB + OWN * c, OWN)]
        pending.append(send(band[g].at[block_of(N_COL - 2 + c)], low, gsem[g]["h"], (wrap(d + 1, N_DOM), q)))
        pending.append(send(band[g].at[block_of(c)], high, gsem[g]["h"] + 1, (wrap(d - 1, N_DOM), q)))

    def slab(g, at_x, half):
        return hub[g].at[pl.ds(NZ * at_x, NZ), pl.ds(HALF * half, HALF)]

    def g_spread(g):
        arrived(hubz.at[g, pl.ds(0, NZ - 1)], gsem[g]["hb"])
        mine = slab(g, x, c)
        for i in (2, 1, 3):
            pending.append(send(hubz.at[g], mine, gsem[g]["hc"] + i, at_xz(i, 0)))
        pending.append(send(hubz.at[g], mine, gsem[g]["hcf"], sib))
        for s in range(NZ):
            hub[g][NZ * x + s, pl.ds(HALF * c, HALF)] = hubz[g, s]

    def g_halo(g):
        for n, at in enumerate((OWN * c, HW + PB + OWN * c)):
            part = band[g].at[pl.ds(at, OWN)]
            arrived(part, gsem[g]["h"] + n)
            pending.append(send(part, part, gsem[g]["h"] + 2 + n, sib))

    def g_panel_end(g):
        arrived(band[g].at[block_of(2 * y + other)], gsem[g]["p"])
        for k in (1, 3, 2):
            arrived(band[g].at[block_of(2 * wrap(y - k, NY) + other)], gsem[g]["pf"] + k)

    def g_halo_end(g):
        arrived(band[g].at[pl.ds(OWN * other, OWN)], gsem[g]["h"] + 2)
        arrived(band[g].at[pl.ds(HW + PB + OWN * other, OWN)], gsem[g]["h"] + 3)

    def g_pass(g):
        for i in (1, 3, 2):
            part = slab(g, wrap(x - i, NX), c)
            arrived(part, gsem[g]["hc"] + i)
            pending.append(send(part, part, gsem[g]["hcf"] + i, sib))

    def g_hub_end(g):
        for i in (0, 1, 3, 2):
            arrived(slab(g, wrap(x - i, NX), other), gsem[g]["hcf"] + i)

    def multiply(g, source, first, count):
        def group(n, total):
            for u in range(8):
                t = first + 8 * n + u
                high, low = split(source[table[t, 1]])
                left = jnp.concatenate(
                    [jnp.concatenate([high, high], axis=1), jnp.concatenate([low, jnp.zeros_like(low)], axis=1)], axis=0
                )
                both = jnp.dot(left, weights[table[t, 0]], preferred_element_type=F32)
                total = total * table[t, 2].astype(F32) + (both[:K] + both[K:])
                prods[g][t] = total
            return total

        lax.fori_loop(0, count // 8, group, jnp.zeros((K, TB), F32))

    def row_sum(g, r):
        return prods[g][table[r, 3]] * table[r, 4].astype(F32) + prods[g][table[r, 5]] * table[r, 6].astype(F32)

    ssems = [(sems(NY), sems(NY)) for _ in range(ITERS)]

    def scatter_start(n, rows_of):
        for k in (2, 1, 3, 0):
            for j, block in enumerate(rows_of(OWN * (2 * wrap(y + k, NY) + other))):
                ssend[n, k, j] = block
            pending.append(send(ssend.at[n, k], srecv.at[n, k], ssems[n][0] + k, sib))
        for k in (2, 1, 3):
            blocks = rows_of(OWN * (2 * wrap(y + k, NY) + c))
            arrived(srecv.at[n, k], ssems[n][0] + k)
            for j, block in enumerate(blocks):
                rsum[n, k, j] = block + srecv[n, k, j]
            pending.append(send(rsum.at[n, k], rrecv.at[n, k], ssems[n][1] + k, at_y(k)))
        return rows_of(OWN * q)

    def scatter_end(n, blocks):
        arrived(srecv.at[n, 0], ssems[n][0])
        blocks = [block + srecv[n, 0, j] for j, block in enumerate(blocks)]
        for k in (1, 3, 2):
            arrived(rrecv.at[n, k], ssems[n][1] + k)
            blocks = [block + rrecv[n, k, j] for j, block in enumerate(blocks)]
        return jnp.concatenate(blocks, axis=1)

    def panel_cross(block_at, groups):
        def some(n, total):
            for u in range(4):
                r = 4 * n + u
                ph, pl_ = split(block_at(r))
                gh, gl = split(jnp.concatenate([band[g][HW + r] for g in groups], axis=0))
                total = total + lax.dot_general(
                    jnp.concatenate([ph, ph, pl_], axis=1), jnp.concatenate([gh, gl, gh], axis=1),
                    (((1,), (1,)), ((), ())), preferred_element_type=F32,
                )
            return total

        return lax.fori_loop(0, PB // 4, some, jnp.zeros((K, K * len(groups)), F32))

    sets = ((pay0, ra0, rb0, rx0, rc0), (pay1, ra1, rb1, rx1, rc1))
    asems = [sems(4) for _ in range(ITERS + 1)]

    def refs(n):
        return [(ref.at[0] if n == 0 else ref.at[n - 1]) for ref in sets[min(n, 1)]]

    def a_start(n, value):
        pay, ra, _, _, _ = refs(n)
        pay[...] = value
        for k in range(1, N_COL):
            peer = wrap(q + k, N_COL)
            send(pay.at[pl.ds(8 * peer, 8)], ra.at[q], asems[n], (d, peer))
        pending.append((ra.at[pl.ds(0, N_COL - 1)], asems[n]))
        ra[q] = pay[pl.ds(8 * q, 8)]

    def a_sum(ref, count, sem):
        arrived(ref.at[pl.ds(0, count - 1)], sem)
        total = ref[0]
        for k in range(1, count):
            total = total + ref[k]
        return total

    def a_z(n):
        _, ra, rb, _, _ = refs(n)
        rb[z] = a_sum(ra, N_COL, asems[n])
        for k in (4, 3, 5, 2, 6, 1, 7):
            send(rb.at[z], rb.at[z], asems[n] + 1, at_xz(0, k))
        pending.append((rb.at[pl.ds(0, NZ - 1)], asems[n] + 1))

    def a_x(n):
        _, _, rb, rx, _ = refs(n)
        rx[x] = a_sum(rb, NZ, asems[n] + 1)
        for i in (2, 1, 3):
            send(rx.at[x], rx.at[x], asems[n] + 2, at_xz(i, 0))
        pending.append((rx.at[pl.ds(0, NX - 1)], asems[n] + 2))

    def a_back(n):
        _, _, _, rx, rc = refs(n)
        rc[q] = a_sum(rx, NX, asems[n] + 2)
        for k in range(1, N_COL):
            send(rc.at[q], rc.at[q], asems[n] + 3, (d, wrap(q + k, N_COL)))
        pending.append((rc.at[pl.ds(0, N_COL - 1)], asems[n] + 3))

    def a_end(n):
        _, _, _, _, rc = refs(n)
        arrived(rc.at[pl.ds(0, N_COL - 1)], asems[n] + 3)
        return jnp.concatenate([rc[k] for k in range(N_COL)], axis=0)

    wsems = [sems(4) for _ in range(ITERS)]

    def w_start(n, w):
        square = nt(w, w)
        wpay[n] = jnp.concatenate([square[: K // 2], square[K // 2 :]], axis=1)
        pending.append(send(wpay.at[n, pl.ds(16 * other, 16)], wrecv.at[n], wsems[n], sib))

    def w_plane(n):
        arrived(wrecv.at[n], wsems[n])
        at = x * NY + y
        wplane[n, at] = wpay[n, pl.ds(16 * c, 16)] + wrecv[n]
        for i, k in ((2, 2), (2, 1), (2, 3), (1, 2), (3, 2), (2, 0), (0, 2), (1, 1), (1, 3), (3, 1), (3, 3), (1, 0), (3, 0), (0, 1), (0, 3)):
            peer = (wrap(x + i, NX) * NZ + z, 2 * wrap(y + k, NY) + c)
            send(wplane.at[n, at], wplane.at[n, at], wsems[n] + 1, peer)
        pending.append((wplane.at[n, pl.ds(0, NX * NY - 1)], wsems[n] + 1))

    def w_z(n):
        wz[n, z] = a_sum(wplane.at[n], NX * NY, wsems[n] + 1)
        for k in (4, 3, 5, 2, 6, 1, 7):
            send(wz.at[n, z], wz.at[n, z], wsems[n] + 2, at_xz(0, k))
        pending.append((wz.at[n, pl.ds(0, NZ - 1)], wsems[n] + 2))

    def w_back(n):
        wend[n, pl.ds(16 * c, 16)] = a_sum(wz.at[n], NZ, wsems[n] + 2)
        half = wend.at[n, pl.ds(16 * c, 16)]
        pending.append(send(half, half, wsems[n] + 3, sib))

    def w_end(n):
        arrived(wend.at[n, pl.ds(16 * other, 16)], wsems[n] + 3)
        whole = wend[n]
        return jnp.concatenate([whole[:, :K], whole[:, K:]], axis=0)

    def prepared(it, gvd, cross):
        coeff = rot[it]
        c1, c2, c3 = coeff[:, 0:K], coeff[:, K : 2 * K], coeff[:, 2 * K :]
        shift = nn(c2, cross[:, :K])
        yall = jnp.concatenate([c1 - shift, c3, c2], axis=1)
        zall = jnp.concatenate([-shift, c3, c2], axis=1)
        upper = jnp.concatenate([gvd, cross], axis=0)
        return yall, zall, upper, nn(yall, upper)

    def coefficients(yall, zall, left, lower):
        reduced = nt(jnp.concatenate([left, nt(yall, lower)], axis=1), yall)
        inverse = eliminate(reduced)
        return jnp.concatenate([nn(inverse, yall), nn(inverse, zall)], axis=0)

    def prepare(t, carry):
        high, low = split(tiles[t].T)
        weights[t, 0:TB] = high
        weights[t, TB:] = low
        return carry

    def prepare_some(n):
        lax.fori_loop(NT // 4 * n, NT // 4 * (n + 1), prepare, 0)

    local[0].wait()
    pl.semaphore_wait(barrier, len(partners))
    g_hub_start(0, masked(xt, 0))
    g_start(0, xt, 0)
    local[1].wait()
    both = xt[0 : 2 * K, :]
    gram = nt(both, both)
    a_start(0, jnp.concatenate([gram[:K], gram[K:]], axis=1))
    table_v[...] = plan(band_rows, band_cols, hub_rows, hub_slots)
    to_smem = pltpu.make_async_copy(table_v, table, lsem.at[5])
    to_smem.start()
    for n in (2, 3, 4):
        local[n].wait()
    prepare_some(0)
    g_hub(0)
    a_z(0)
    prepare_some(1)
    g_panel(0)
    g_hub_start(1, masked(xt, K))
    g_start(1, xt, K)
    prepare_some(2)
    g_spread(0)
    prepare_some(3)
    a_x(0)
    g_hub(1)
    to_smem.wait()
    g_halo(0)
    g_panel_end(0)
    g_halo_end(0)
    multiply(0, band[0], 0, TPD)
    g_panel(1)
    a_back(0)
    g_pass(0)
    g_hub_end(0)
    multiply(0, hub[0], TPD, HTD)

    def first_rows(r):
        return [row_sum(0, r + j) for j in range(OWN)]

    g_hub_start(2, row_sum(0, hub_row))
    kept = scatter_start(0, first_rows)
    g_spread(1)
    g_panel_end(1)
    a_start(1, panel_cross(lambda r: row_sum(0, r), (0, 1)))
    g_hub(2, hub[0][d, pl.ds(HALF * c, HALF)])
    g_halo(1)
    sums = a_end(0)
    gvd = jnp.concatenate([sums[:, : 2 * K], sums[:, 2 * K :]], axis=0)
    w = xt[0:K] - scatter_end(0, kept)
    xt[2 * K :] = w
    w_start(0, w)
    g_start(2, xt, 2 * K)
    w_plane(0)
    a_z(1)
    g_spread(2)
    g_halo_end(1)
    multiply(1, band[1], 0, TPD)
    g_pass(1)
    w_z(0)
    a_x(1)
    g_panel(2)
    g_hub_end(1)
    multiply(1, hub[1], TPD, HTD)
    a_back(1)
    w_back(0)
    g_halo(2)
    cross = gvd[:K] - a_end(1)
    yall, zall, upper, left = prepared(0, gvd, cross)
    g_pass(2)
    lower = jnp.concatenate([cross, w_end(0)], axis=1)
    mix = coefficients(yall, zall, left, lower)
    mix_high, mix_low = split(mix[:K])
    mix_both = jnp.concatenate([mix_high, mix_low], axis=0)
    g_panel_end(2)
    g_halo_end(2)
    multiply(2, band[2], 0, TPD)
    g_hub_end(2)
    multiply(2, hub[2], TPD, HTD)

    def second_rows(r):
        stack = jnp.concatenate(
            [jnp.concatenate([row_sum(g, r + j) for j in range(OWN)], axis=1) for g in range(3)], axis=0
        )
        high, low = split(stack)
        one = jnp.dot(mix_both, high, preferred_element_type=F32)
        two = jnp.dot(mix_high, low, preferred_element_type=F32)
        out = one[:K] + one[K:] + two
        blocks = [out[:, TB * j : TB * (j + 1)] for j in range(OWN)]
        for j in range(OWN):
            mixed[r + j] = blocks[j]
        return blocks

    kept = scatter_start(1, second_rows)
    a_start(2, nt(panel_cross(lambda r: mixed[r], (0, 1, 2)), mix[:, : K * 3]))
    xt2[0 : 2 * K] = nn(mix, xt[...])
    carried = jnp.concatenate([nn(mix, upper), nt(mix, lower)], axis=1)
    gvd = nt(carried, mix)
    w = xt2[0:K] - scatter_end(1, kept)
    xt2[2 * K :] = w
    w_start(1, w)
    a_z(2)
    w_plane(1)
    a_x(2)
    w_z(1)
    a_back(2)
    w_back(1)
    cross = gvd[:K] - a_end(2)
    ritz_out[...] = cross[:, :K]
    yall, zall, upper, left = prepared(1, gvd, cross)
    mix_out[...] = coefficients(yall, zall, left, jnp.concatenate([cross, w_end(1)], axis=1))

    for item in pending:
        if isinstance(item, tuple):
            ref, sem = item
            pltpu.make_async_copy(ref, ref, ssem.at[sem]).wait()
        else:
            item.wait_send()


def finish(mix, state, ritz, vec_out, dir_out, ritz_out):
    whole = state[...]
    vec_out[...] = nn(mix[:K], whole)
    dir_out[...] = nn(mix[K:], whole)
    ritz_out[...] = ritz[...].T


def per_device(
    band_tiles, band_rows, band_cols, hub_tiles, hub_rows, hub_slots, hub_blocks,
    start_vectors, prior_directions, rotation,
):
    smem = pl.BlockSpec(memory_space=pltpu.SMEM)
    vmem = pl.BlockSpec(memory_space=pltpu.VMEM)
    hbm = pl.BlockSpec(memory_space=pltpu.HBM)
    rows = start_vectors.shape[0]
    ext = [pltpu.VMEM((EXT, K, TB), F32)] * 3 + [pltpu.VMEM((HUBS, K, TB), F32)] * 3
    mix, state, ritz = pl.pallas_call(
        kernel,
        out_shape=(
            jax.ShapeDtypeStruct((2 * K, 3 * K), F32),
            jax.ShapeDtypeStruct((3 * K, rows), F32),
            jax.ShapeDtypeStruct((K, K), F32),
        ),
        in_specs=[smem] * 5 + [hbm] * 5,
        out_specs=(vmem, vmem, vmem),
        scratch_shapes=[
            pltpu.VMEM((NT, TB, TB), F32),
            pltpu.VMEM((NT, 2 * TB, TB), BF16),
            pltpu.VMEM((NT, TB), jnp.int32),
            pltpu.SMEM((NT, TB), jnp.int32),
            pltpu.VMEM((ITERS, K, 3 * K), F32),
            pltpu.VMEM((3 * K, rows), F32),
            pltpu.VMEM((3, OWN, K, TB), F32),
            pltpu.VMEM((3, K, TB), F32),
            pltpu.VMEM((3, N_COL, HALF, TB), F32),
            pltpu.VMEM((3, NZ, HALF, TB), F32),
            *ext,
            *[pltpu.VMEM((NT, K, TB), F32)] * 3,
            pltpu.VMEM((PB, K, TB), F32),
            *[pltpu.VMEM((ITERS, NY, OWN, K, TB), F32)] * 4,
            *[
                pltpu.VMEM((count,) + shape + (width,), F32)
                for count, width in ((1, 4 * K), (ITERS, 2 * K))
                for shape in ((K,), (N_COL, 8), (NZ, 8), (NX, 8), (N_COL, 8))
            ],
            pltpu.VMEM((ITERS, K // 2, 2 * K), F32),
            pltpu.VMEM((ITERS, K // 4, 2 * K), F32),
            pltpu.VMEM((ITERS, NX * NY, K // 4, 2 * K), F32),
            pltpu.VMEM((ITERS, NZ, K // 4, 2 * K), F32),
            pltpu.VMEM((ITERS, K // 2, 2 * K), F32),
            pltpu.SemaphoreType.DMA((6,)),
            pltpu.SemaphoreType.DMA((120,)),
            pltpu.SemaphoreType.DMA((120,)),
        ],
        compiler_params=pltpu.CompilerParams(
            collective_id=0, has_side_effects=True, vmem_limit_bytes=56 * 1024 * 1024
        ),
        name="lobpcg",
    )(
        band_rows, band_cols, hub_rows, hub_slots, hub_blocks, start_vectors.T, prior_directions.T,
        jnp.transpose(rotation, (0, 2, 1)), band_tiles, hub_tiles,
    )
    vec, direc, ritz = pl.pallas_call(
        finish,
        out_shape=(
            jax.ShapeDtypeStruct((K, rows), F32),
            jax.ShapeDtypeStruct((K, rows), F32),
            jax.ShapeDtypeStruct((K, K), F32),
        ),
        in_specs=[vmem] * 3,
        out_specs=(vmem, vmem, vmem),
        name="finish",
    )(mix, state, ritz)
    return vec.T, direc.T, ritz


def solution(mesh):
    return jax.shard_map(
        per_device,
        mesh=mesh,
        in_specs=(
            P(("dom", "col"), None, None),
            P(("dom", "col")),
            P(("dom", "col")),
            P(("dom", "col"), None, None),
            P(("dom", "col")),
            P(("dom", "col")),
            P(),
            P(("dom", "col"), None),
            P(("dom", "col"), None),
            P(),
        ),
        out_specs=(P(("dom", "col"), None), P(("dom", "col"), None), P()),
        check_vma=False,
    )
```

```python
import jax
import jax.numpy as jnp
from jax import lax
from jax.experimental import pallas as pl
from jax.experimental.pallas import tpu as pltpu
from jax.sharding import PartitionSpec as P

TB = 128
K = 64
PB = 32
ITERS = 2
HW = 8
NZ = 8
NX = 4
NY = 4
N_DOM = 32
N_COL = 8
TPD = 24
HTD = 8
NT = TPD + HTD
OWN = 4
EXT = PB + 2 * HW
HUBS = 32
HALF = 32
MESH = pl.DeviceIdType.MESH
F32 = jnp.float32
BF16 = jnp.bfloat16
HI = lax.Precision.HIGHEST


def wrap(value, count):
    return lax.rem(value + count, count)


def nn(a, b):
    return jnp.dot(a, b, precision=HI, preferred_element_type=F32)


def nt(a, b):
    return lax.dot_general(a, b, (((1,), (1,)), ((), ())), precision=HI, preferred_element_type=F32)


def split(value):
    high = value.astype(BF16)
    return high, (value - high.astype(F32)).astype(BF16)


def eliminate(matrix):
    full = (8, 2 * K)
    rows = lax.broadcasted_iota(jnp.int32, full, 0)
    lanes = lax.broadcasted_iota(jnp.int32, full, 1)
    wide = jnp.concatenate([matrix, jnp.zeros((K, K), F32)], axis=1)
    blocks = [jnp.where(lanes - K == rows + 8 * b, 1.0, wide[8 * b : 8 * b + 8]) for b in range(K // 8)]
    for home in range(K // 8):
        cols = [
            [jnp.broadcast_to(blocks[b][:, 8 * home + c : 8 * home + c + 1], full) for c in range(8)]
            for b in range(home, K // 8)
        ]
        work = [jnp.broadcast_to(blocks[home][r : r + 1, :], full) for r in range(8)]
        a = [[jnp.broadcast_to(cols[0][c][r : r + 1, :], full) for c in range(r + 1)] for r in range(8)]
        scale, done = [], []
        for c in range(8):
            scale.append(lax.rsqrt(a[c][c]))
            done.append(work[c] * scale[c])
            for r in range(c + 1, 8):
                a[r][c] = a[r][c] * scale[c]
            for r in range(c + 1, 8):
                for e in range(c + 1, r + 1):
                    a[r][e] = a[r][e] - a[r][c] * a[e][c]
                work[r] = work[r] - a[r][c] * done[c]
        back = [None] * 8
        for c in reversed(range(8)):
            value = done[c]
            for r in range(c + 1, 8):
                value = value - a[r][c] * back[r]
            back[c] = value * scale[c]
        for b in range(home + 1, K // 8):
            for c in range(8):
                blocks[b] = blocks[b] - cols[b - home][c] * back[c]
        for r in range(8):
            blocks[home] = jnp.where(rows == r, done[r], blocks[home])
    return jnp.concatenate(blocks, axis=0)[:, K:]


def plan(band_rows, band_cols, hub_rows, hub_slots):
    full = (NT, TB)
    sub = lax.broadcasted_iota(jnp.int32, full, 0)
    lane = lax.broadcasted_iota(jnp.int32, full, 1)
    key_s = jnp.zeros(full, jnp.int32)
    key_l = jnp.full(full, 4 * PB, jnp.int32)
    src_l = jnp.zeros(full, jnp.int32)
    for t in range(NT):
        key = band_rows[t] if t < TPD else PB + hub_rows[t - TPD]
        src = band_cols[t] if t < TPD else hub_slots[t - TPD]
        key_s = jnp.where(sub == t, key, key_s)
        key_l = jnp.where(lane == t, key, key_l)
        src_l = jnp.where(lane == t, src, src_l)

    def one(cond):
        return jnp.where(cond, 1, 0)

    same = jnp.where(sub < lane, one(key_s == key_l), 0)
    place = jnp.sum(one(key_s < key_l) + same, axis=0, keepdims=True)
    again = jnp.sum(same, axis=0, keepdims=True)
    place = jnp.where(lane < NT, jnp.broadcast_to(place, full), NT)
    chosen = one(place == sub)

    def across(value):
        return jnp.sum(value, axis=1, keepdims=True)

    columns = [
        across(chosen * lane),
        across(chosen * src_l),
        across(chosen * one(jnp.broadcast_to(again, full) > 0)),
        jnp.maximum(across(one(key_l <= sub)) - 1, 0),
        one(across(one(key_l == sub)) > 0),
        jnp.maximum(across(one(key_l <= sub + PB)) - 1, 0),
        one(across(one(key_l == sub + PB)) > 0),
    ]
    table = jnp.zeros(full, jnp.int32)
    for n, column in enumerate(columns):
        table = jnp.where(lane == n, jnp.broadcast_to(column, full), table)
    return table


def kernel(
    blocks_hbm, rows_hbm, cols_hbm, hrows_hbm, slots_hbm, vec_hbm, dir_hbm, rot_hbm, band_hbm, hub_hbm,
    mix_out, xt2, ritz_out,
    hub_blocks, band_rows, band_cols, hub_rows, hub_slots,
    tiles, weights, table_v, table, rot, xt,
    own, cand, hca, hubz, eb0, eb1, eb2, eh0, eh1, eh2, pr0, pr1, pr2, mixed,
    ssend, srecv, rsum, rrecv, pay0, ra0, rb0, rx0, rc0, pay1, ra1, rb1, rx1, rc1,
    wpay, wrecv, wplane, wz, wend, lsem, ssem, rsem,
):
    d = lax.axis_index("dom")
    q = lax.axis_index("col")
    x, z = d // NZ, d % NZ
    y, c = q // 2, q % 2
    other = 1 - c
    sib = (d, q + 1 - 2 * c)
    band, hub, prods = (eb0, eb1, eb2), (eh0, eh1, eh2), (pr0, pr1, pr2)

    def at_y(k):
        return (d, 2 * wrap(y + k, NY) + c)

    def at_xz(i, k):
        return (wrap(x + i, NX) * NZ + wrap(z + k, NZ), q)

    def at_xy(i, k):
        return (wrap(x + i, NX) * NZ + z, 2 * wrap(y + k, NY) + c)

    plane = ((2, 2), (2, 1), (2, 3), (1, 2), (3, 2), (2, 0), (0, 2), (1, 1), (1, 3), (3, 1), (3, 3), (1, 0), (3, 0), (0, 1), (0, 3))
    partners = [at_xz(0, k) for k in (4, 3, 5, 2, 6, 1, 7)] + [at_xz(i, 0) for i in (2, 1, 3)]
    partners += [(wrap(d + 1, N_DOM), q), (wrap(d - 1, N_DOM), q)] + [(d, wrap(q + k, N_COL)) for k in range(1, N_COL)]

    barrier = pltpu.get_barrier_semaphore()
    for partner in partners:
        pl.semaphore_signal(barrier, inc=1, device_id=partner, device_id_type=MESH)

    local = []
    for n, (src, dst) in enumerate(
        (
            (blocks_hbm, hub_blocks),
            (vec_hbm, xt.at[pl.ds(0, K)]),
            (rows_hbm, band_rows),
            (cols_hbm, band_cols),
            (hrows_hbm, hub_rows),
            (slots_hbm, hub_slots),
            (dir_hbm, xt.at[pl.ds(K, K)]),
            (band_hbm, tiles.at[pl.ds(0, TPD)]),
            (hub_hbm, tiles.at[pl.ds(TPD, HTD)]),
            (rot_hbm, rot),
        )
    ):
        local.append(pltpu.make_async_copy(src, dst, lsem.at[n]))
        local[n].start()
    counter = [0]
    pending = []

    def sems(n=1):
        counter[0] += n
        return counter[0] - n

    def drain():
        for item in pending:
            if isinstance(item, tuple):
                ref, sem = item
                pltpu.make_async_copy(ref, ref, ssem.at[sem]).wait()
            else:
                item.wait_send()
        pending.clear()

    def send(src, dst, sem, device):
        copy = pltpu.make_async_remote_copy(
            src_ref=src, dst_ref=dst, send_sem=ssem.at[sem], recv_sem=rsem.at[sem],
            device_id=device, device_id_type=MESH,
        )
        copy.start()
        return copy

    def arrived(ref, sem):
        pltpu.make_async_copy(ref, ref, rsem.at[sem]).wait()

    def block_of(col):
        return pl.ds(HW + OWN * col, OWN)

    local[0].wait()
    mask = [jnp.where(hub_blocks[d] - d * PB - q * OWN == j, 1.0, 0.0) for j in range(OWN)]
    names = ("ha", "p", "hb", "pf", "h", "hc", "hcf")
    gsem = [dict(zip(names, [sems(n) for n in (1, NY, NZ, NY, 4, NX, NX)])) for _ in range(3)]
    hub_row = jnp.clip(hub_blocks[d] - d * PB, 0, PB - 1)

    def g_start(g, ref, first):
        for j in range(OWN):
            block = ref[first : first + K, TB * j : TB * (j + 1)]
            own[g, j] = block
            band[g][HW + OWN * q + j] = block
        mine = band[g].at[block_of(q)]
        for k in (2, 1, 3):
            pending.append(send(own.at[g], mine, gsem[g]["p"] + k, at_y(k)))
        pending.append(send(own.at[g], mine, gsem[g]["p"], sib))

    def masked(ref, first):
        pick = jnp.zeros((K, TB), F32)
        for j in range(OWN):
            pick = pick + ref[first : first + K, TB * j : TB * (j + 1)] * mask[j]
        return pick

    def g_hub_start(g, term):
        cand[g] = term
        for k in range(1, N_COL):
            peer = wrap(q + k, N_COL)
            send(cand.at[g, pl.ds(HALF * (peer % 2), HALF)], hca.at[g, q], gsem[g]["ha"], (d, peer))
        pending.append((hca.at[g, pl.ds(0, N_COL - 1)], gsem[g]["ha"]))
        hca[g, q] = cand[g, pl.ds(HALF * c, HALF)]

    def g_hub(g, base=None):
        arrived(hca.at[g, pl.ds(0, N_COL - 1)], gsem[g]["ha"])
        piece = hca[g, 0]
        for k in range(1, N_COL):
            piece = piece + hca[g, k]
        hubz[g, z] = piece if base is None else base - piece
        for k in (4, 3, 5, 2, 6, 1, 7):
            pending.append(send(hubz.at[g, z], hubz.at[g, z], gsem[g]["hb"] + k, at_xz(0, k)))
        hub_on(g, z)

    def g_panel(g):
        for k in (1, 3, 2):
            block = band[g].at[block_of(2 * wrap(y - k, NY) + c)]
            arrived(block, gsem[g]["p"] + k)
            pending.append(send(block, block, gsem[g]["pf"] + k, sib))
        low, high = band[g].at[pl.ds(OWN * c, OWN)], band[g].at[pl.ds(HW + PB + OWN * c, OWN)]
        pending.append(send(band[g].at[block_of(N_COL - 2 + c)], low, gsem[g]["h"], (wrap(d + 1, N_DOM), q)))
        pending.append(send(band[g].at[block_of(c)], high, gsem[g]["h"] + 1, (wrap(d - 1, N_DOM), q)))

    def slab(g, at_x, half):
        return hub[g].at[pl.ds(NZ * at_x, NZ), pl.ds(HALF * half, HALF)]

    def hub_on(g, at_z):
        mine = hub[g].at[NZ * x + at_z, pl.ds(HALF * c, HALF)]
        for i in (2, 1, 3):
            send(hubz.at[g, at_z], mine, gsem[g]["hc"] + i, at_xz(i, 0))
        hub[g][NZ * x + at_z, pl.ds(HALF * c, HALF)] = hubz[g, at_z]

    def g_spread(g, part=None):
        near = (1, 7, 2, 6), (3, 5, 4)
        for k in near[0] + near[1] if part is None else near[part]:
            at_z = wrap(z - k, NZ)
            arrived(hubz.at[g, at_z], gsem[g]["hb"] + k)
            hub_on(g, at_z)
        if part != 0:
            pending.extend((hubz.at[g], gsem[g]["hc"] + i) for i in (1, 2, 3))
            pending.append(send(hubz.at[g], slab(g, x, c), gsem[g]["hcf"], sib))

    def g_halo(g):
        for n, at in enumerate((OWN * c, HW + PB + OWN * c)):
            part = band[g].at[pl.ds(at, OWN)]
            arrived(part, gsem[g]["h"] + n)
            pending.append(send(part, part, gsem[g]["h"] + 2 + n, sib))

    def g_panel_end(g):
        arrived(band[g].at[block_of(2 * y + other)], gsem[g]["p"])
        for k in (1, 3, 2):
            arrived(band[g].at[block_of(2 * wrap(y - k, NY) + other)], gsem[g]["pf"] + k)

    def g_halo_end(g):
        arrived(band[g].at[pl.ds(OWN * other, OWN)], gsem[g]["h"] + 2)
        arrived(band[g].at[pl.ds(HW + PB + OWN * other, OWN)], gsem[g]["h"] + 3)

    def g_pass(g):
        for i in (1, 3, 2):
            part = slab(g, wrap(x - i, NX), c)
            arrived(part, gsem[g]["hc"] + i)
            pending.append(send(part, part, gsem[g]["hcf"] + i, sib))

    def g_hub_end(g):
        for i in (0, 1, 3, 2):
            arrived(slab(g, wrap(x - i, NX), other), gsem[g]["hcf"] + i)

    def multiply(g, source, first, count):
        def group(n, total):
            for u in range(8):
                t = first + 8 * n + u
                high, low = split(source[table[t, 1]])
                left = jnp.concatenate(
                    [jnp.concatenate([high, high], axis=1), jnp.concatenate([low, jnp.zeros_like(low)], axis=1)], axis=0
                )
                both = jnp.dot(left, weights[table[t, 0]], preferred_element_type=F32)
                product = both[:K] + both[K:]
                total = total * table[t, 2].astype(F32) + product
                prods[g][t] = total
            return total

        lax.fori_loop(0, count // 8, group, jnp.zeros((K, TB), F32))

    def row_sum(g, r):
        return prods[g][table[r, 3]] * table[r, 4].astype(F32) + prods[g][table[r, 5]] * table[r, 6].astype(F32)

    ssems = [(sems(NY), sems(NY)) for _ in range(ITERS)]

    def scatter_start(n, rows_of):
        for k in (2, 1, 3, 0):
            for j, block in enumerate(rows_of(OWN * (2 * wrap(y + k, NY) + other))):
                ssend[n, k, j] = block
            pending.append(send(ssend.at[n, k], srecv.at[n, k], ssems[n][0] + k, sib))
        for k in (2, 1, 3):
            blocks = rows_of(OWN * (2 * wrap(y + k, NY) + c))
            arrived(srecv.at[n, k], ssems[n][0] + k)
            for j, block in enumerate(blocks):
                rsum[n, k, j] = block + srecv[n, k, j]
            pending.append(send(rsum.at[n, k], rrecv.at[n, k], ssems[n][1] + k, at_y(k)))
        return rows_of(OWN * q)

    def scatter_end(n, blocks):
        arrived(srecv.at[n, 0], ssems[n][0])
        blocks = [block + srecv[n, 0, j] for j, block in enumerate(blocks)]
        for k in (1, 3, 2):
            arrived(rrecv.at[n, k], ssems[n][1] + k)
            blocks = [block + rrecv[n, k, j] for j, block in enumerate(blocks)]
        return jnp.concatenate(blocks, axis=1)

    def cross_of(blocks, groups, at):
        highs, lows = zip(*[split(block) for block in blocks])
        there = [split(jnp.concatenate([band[g][HW + r] for g in groups], axis=0)) for r in at]
        left, right = [], []
        for ph, pl_, (gh, gl) in zip(highs, lows, there):
            left += [ph, ph, pl_]
            right += [gh, gl, gh]
        return lax.dot_general(
            jnp.concatenate(left, axis=1), jnp.concatenate(right, axis=1), (((1,), (1,)), ((), ())),
            preferred_element_type=F32,
        )

    def panel_cross(block_at, groups):
        def some(n, total):
            for u in range(0, 4, 2):
                at = (4 * n + u, 4 * n + u + 1)
                total = total + cross_of([block_at(r) for r in at], groups, at)
            return total

        return lax.fori_loop(0, PB // 4, some, jnp.zeros((K, K * len(groups)), F32))

    sets = ((pay0, ra0, rb0, rx0, rc0), (pay1, ra1, rb1, rx1, rc1))
    asems = [sems(4) for _ in range(ITERS + 1)]

    def refs(n):
        return [(ref.at[0] if n == 0 else ref.at[n - 1]) for ref in sets[min(n, 1)]]

    def a_start(n, value):
        pay, ra, _, _, _ = refs(n)
        pay[...] = value
        for k in range(1, N_COL):
            peer = wrap(q + k, N_COL)
            send(pay.at[pl.ds(8 * peer, 8)], ra.at[q], asems[n], (d, peer))
        pending.append((ra.at[pl.ds(0, N_COL - 1)], asems[n]))
        ra[q] = pay[pl.ds(8 * q, 8)]

    def a_sum(ref, count, sem):
        arrived(ref.at[pl.ds(0, count - 1)], sem)
        total = ref[0]
        for k in range(1, count):
            total = total + ref[k]
        return total

    def a_z(n):
        _, ra, rb, _, _ = refs(n)
        rb[z] = a_sum(ra, N_COL, asems[n])
        for k in (4, 3, 5, 2, 6, 1, 7):
            send(rb.at[z], rb.at[z], asems[n] + 1, at_xz(0, k))
        pending.append((rb.at[pl.ds(0, NZ - 1)], asems[n] + 1))

    def a_x(n):
        _, _, rb, rx, _ = refs(n)
        rx[x] = a_sum(rb, NZ, asems[n] + 1)
        for i in (2, 1, 3):
            send(rx.at[x], rx.at[x], asems[n] + 2, at_xz(i, 0))
        pending.append((rx.at[pl.ds(0, NX - 1)], asems[n] + 2))

    def a_back(n):
        _, _, _, rx, rc = refs(n)
        rc[q] = a_sum(rx, NX, asems[n] + 2)
        for k in range(1, N_COL):
            send(rc.at[q], rc.at[q], asems[n] + 3, (d, wrap(q + k, N_COL)))
        pending.append((rc.at[pl.ds(0, N_COL - 1)], asems[n] + 3))

    def a_end(n):
        _, _, _, _, rc = refs(n)
        arrived(rc.at[pl.ds(0, N_COL - 1)], asems[n] + 3)
        return jnp.concatenate([rc[k] for k in range(N_COL)], axis=0)

    wsems = [sems(4) for _ in range(ITERS)]

    def w_start(n, w):
        square = nt(w, w)
        wpay[n] = jnp.concatenate([square[: K // 2], square[K // 2 :]], axis=1)
        pending.append(send(wpay.at[n, pl.ds(16 * other, 16)], wrecv.at[n], wsems[n], sib))

    def w_plane(n):
        arrived(wrecv.at[n], wsems[n])
        at = x * NY + y
        wplane[n, at] = wpay[n, pl.ds(16 * c, 16)] + wrecv[n]
        for i, k in plane:
            send(wplane.at[n, at], wplane.at[n, at], wsems[n] + 1, at_xy(i, k))
        pending.append((wplane.at[n, pl.ds(0, NX * NY - 1)], wsems[n] + 1))

    def w_z(n):
        wz[n, z] = a_sum(wplane.at[n], NX * NY, wsems[n] + 1)
        for k in (4, 3, 5, 2, 6, 1, 7):
            send(wz.at[n, z], wz.at[n, z], wsems[n] + 2, at_xz(0, k))
        pending.append((wz.at[n, pl.ds(0, NZ - 1)], wsems[n] + 2))

    def w_back(n):
        wend[n, pl.ds(16 * c, 16)] = a_sum(wz.at[n], NZ, wsems[n] + 2)
        half = wend.at[n, pl.ds(16 * c, 16)]
        pending.append(send(half, half, wsems[n] + 3, sib))

    def w_end(n):
        arrived(wend.at[n, pl.ds(16 * other, 16)], wsems[n] + 3)
        whole = wend[n]
        return jnp.concatenate([whole[:, :K], whole[:, K:]], axis=0)

    def prepared(it, gvd, cross):
        coeff = rot[it]
        c1, c2, c3 = coeff[:, 0:K], coeff[:, K : 2 * K], coeff[:, 2 * K :]
        shift = nn(c2, cross[:, :K])
        yall = jnp.concatenate([c1 - shift, c3, c2], axis=1)
        zall = jnp.concatenate([-shift, c3, c2], axis=1)
        upper = jnp.concatenate([gvd, cross], axis=0)
        return yall, zall, upper, nn(yall, upper)

    def coefficients(yall, zall, left, lower):
        reduced = nt(jnp.concatenate([left, nt(yall, lower)], axis=1), yall)
        inverse = eliminate(reduced)
        return jnp.concatenate([nn(inverse, yall), nn(inverse, zall)], axis=0)

    def prepare(t, carry):
        high, low = split(tiles[t].T)
        weights[t, 0:TB] = high
        weights[t, TB:] = low
        return carry

    def prepare_some(n):
        lax.fori_loop(NT // 4 * n, NT // 4 * (n + 1), prepare, 0)

    local[1].wait()
    pl.semaphore_wait(barrier, len(partners))
    g_hub_start(0, masked(xt, 0))
    g_start(0, xt, 0)
    local[6].wait()
    both = xt[0 : 2 * K, :]
    gram = nt(both, both)
    a_start(0, jnp.concatenate([gram[:K], gram[K:]], axis=1))
    for n in (2, 3, 4, 5):
        local[n].wait()
    table_v[...] = plan(band_rows, band_cols, hub_rows, hub_slots)
    to_smem = pltpu.make_async_copy(table_v, table, lsem.at[10])
    to_smem.start()
    for n in (7, 8, 9):
        local[n].wait()
    prepare_some(0)
    g_hub(0)
    prepare_some(1)
    a_z(0)
    g_panel(0)
    g_spread(0, 0)
    g_hub_start(1, masked(xt, K))
    g_start(1, xt, K)
    prepare_some(2)
    g_spread(0, 1)
    a_x(0)
    to_smem.wait()
    g_halo(0)
    g_panel_end(0)
    g_halo_end(0)
    multiply(0, band[0], 0, TPD)
    prepare_some(3)
    g_pass(0)
    g_hub(1)
    g_panel(1)
    a_back(0)
    g_hub_end(0)
    multiply(0, hub[0], TPD, HTD)

    def first_rows(r):
        return [row_sum(0, r + j) for j in range(OWN)]

    kept = scatter_start(0, first_rows)
    g_hub_start(2, row_sum(0, hub_row))
    g_panel_end(1)
    a_start(1, panel_cross(lambda r: row_sum(0, r), (0, 1)))
    g_hub(2, hub[0][d, pl.ds(HALF * c, HALF)])
    g_spread(1)
    g_halo(1)
    sums = a_end(0)
    gvd = jnp.concatenate([sums[:, : 2 * K], sums[:, 2 * K :]], axis=0)
    a_z(1)
    w = xt[0:K] - scatter_end(0, kept)
    xt[2 * K :] = w
    w_start(0, w)
    g_start(2, xt, 2 * K)
    w_plane(0)
    g_halo_end(1)
    multiply(1, band[1], 0, TPD)
    a_x(1)
    g_spread(2)
    g_pass(1)
    g_hub_end(1)
    multiply(1, hub[1], TPD, HTD)
    a_back(1)
    w_z(0)
    g_panel(2)
    cross = gvd[:K] - a_end(1)
    yall, zall, upper, left = prepared(0, gvd, cross)
    w_back(0)
    g_pass(2)
    g_halo(2)
    lower = jnp.concatenate([cross, w_end(0)], axis=1)
    mix = coefficients(yall, zall, left, lower)
    mix_high, mix_low = split(mix[:K])
    mix_both = jnp.concatenate([mix_high, mix_low], axis=0)
    g_panel_end(2)
    g_halo_end(2)
    multiply(2, band[2], 0, TPD)
    g_hub_end(2)
    multiply(2, hub[2], TPD, HTD)

    def second_rows(r):
        stack = jnp.concatenate(
            [jnp.concatenate([row_sum(g, r + j) for j in range(OWN)], axis=1) for g in range(3)], axis=0
        )
        high, low = split(stack)
        one = jnp.dot(mix_both, high, preferred_element_type=F32)
        two = jnp.dot(mix_high, low, preferred_element_type=F32)
        out = one[:K] + one[K:] + two
        blocks = [out[:, TB * j : TB * (j + 1)] for j in range(OWN)]
        for j in range(OWN):
            mixed[r + j] = blocks[j]
        return blocks

    kept = scatter_start(1, second_rows)
    a_start(2, nt(panel_cross(lambda r: mixed[r], (0, 1, 2)), mix[:, : K * 3]))
    xt2[0 : 2 * K] = nn(mix, xt[...])
    carried = jnp.concatenate([nn(mix, upper), nt(mix, lower)], axis=1)
    gvd = nt(carried, mix)
    drain()
    a_z(2)
    w = xt2[0:K] - scatter_end(1, kept)
    xt2[2 * K :] = w
    w_start(1, w)
    w_plane(1)
    a_x(2)
    w_z(1)
    a_back(2)
    w_back(1)
    cross = gvd[:K] - a_end(2)
    ritz_out[...] = cross[:, :K]
    yall, zall, upper, left = prepared(1, gvd, cross)
    drain()
    mix_out[...] = coefficients(yall, zall, left, jnp.concatenate([cross, w_end(1)], axis=1))

    drain()


def finish(mix, state, ritz, vec_out, dir_out, ritz_out):
    whole = state[...]
    vec_out[...] = nn(mix[:K], whole)
    dir_out[...] = nn(mix[K:], whole)
    ritz_out[...] = ritz[...].T


def per_device(
    band_tiles, band_rows, band_cols, hub_tiles, hub_rows, hub_slots, hub_blocks,
    start_vectors, prior_directions, rotation,
):
    vmem = pl.BlockSpec(memory_space=pltpu.VMEM)
    hbm = pl.BlockSpec(memory_space=pltpu.HBM)
    rows = start_vectors.shape[0]
    ext = [pltpu.VMEM((EXT, K, TB), F32)] * 3 + [pltpu.VMEM((HUBS, K, TB), F32)] * 3
    mix, state, ritz = pl.pallas_call(
        kernel,
        out_shape=(
            jax.ShapeDtypeStruct((2 * K, 3 * K), F32),
            jax.ShapeDtypeStruct((3 * K, rows), F32),
            jax.ShapeDtypeStruct((K, K), F32),
        ),
        in_specs=[hbm] * 10,
        out_specs=(vmem, vmem, vmem),
        scratch_shapes=[
            *[pltpu.SMEM((count,), jnp.int32) for count in (HUBS, TPD, TPD, HTD, HTD)],
            pltpu.VMEM((NT, TB, TB), F32),
            pltpu.VMEM((NT, 2 * TB, TB), BF16),
            pltpu.VMEM((NT, TB), jnp.int32),
            pltpu.SMEM((NT, TB), jnp.int32),
            pltpu.VMEM((ITERS, K, 3 * K), F32),
            pltpu.VMEM((3 * K, rows), F32),
            pltpu.VMEM((3, OWN, K, TB), F32),
            pltpu.VMEM((3, K, TB), F32),
            pltpu.VMEM((3, N_COL, HALF, TB), F32),
            pltpu.VMEM((3, NZ, HALF, TB), F32),
            *ext,
            *[pltpu.VMEM((NT, K, TB), F32)] * 3,
            pltpu.VMEM((PB, K, TB), F32),
            *[pltpu.VMEM((ITERS, NY, OWN, K, TB), F32)] * 4,
            *[
                pltpu.VMEM((count,) + shape + (width,), F32)
                for count, width in ((1, 4 * K), (ITERS, 2 * K))
                for shape in ((K,), (N_COL, 8), (NZ, 8), (NX, 8), (N_COL, 8))
            ],
            pltpu.VMEM((ITERS, K // 2, 2 * K), F32),
            pltpu.VMEM((ITERS, K // 4, 2 * K), F32),
            pltpu.VMEM((ITERS, NX * NY, K // 4, 2 * K), F32),
            pltpu.VMEM((ITERS, NZ, K // 4, 2 * K), F32),
            pltpu.VMEM((ITERS, K // 2, 2 * K), F32),
            pltpu.SemaphoreType.DMA((11,)),
            pltpu.SemaphoreType.DMA((128,)),
            pltpu.SemaphoreType.DMA((128,)),
        ],
        compiler_params=pltpu.CompilerParams(
            collective_id=0, has_side_effects=True, vmem_limit_bytes=56 * 1024 * 1024
        ),
        name="lobpcg",
    )(
        hub_blocks, band_rows, band_cols, hub_rows, hub_slots, start_vectors.T, prior_directions.T,
        jnp.transpose(rotation, (0, 2, 1)), band_tiles, hub_tiles,
    )
    vec, direc, ritz = pl.pallas_call(
        finish,
        out_shape=(
            jax.ShapeDtypeStruct((K, rows), F32),
            jax.ShapeDtypeStruct((K, rows), F32),
            jax.ShapeDtypeStruct((K, K), F32),
        ),
        in_specs=[vmem] * 3,
        out_specs=(vmem, vmem, vmem),
        name="finish",
    )(mix, state, ritz)
    return vec.T, direc.T, ritz


def solution(mesh):
    return jax.shard_map(
        per_device,
        mesh=mesh,
        in_specs=(
            P(("dom", "col"), None, None),
            P(("dom", "col")),
            P(("dom", "col")),
            P(("dom", "col"), None, None),
            P(("dom", "col")),
            P(("dom", "col")),
            P(),
            P(("dom", "col"), None),
            P(("dom", "col"), None),
            P(),
        ),
        out_specs=(P(("dom", "col"), None), P(("dom", "col"), None), P()),
        check_vma=False,
    )
```

```python
import jax
import jax.numpy as jnp
from jax import lax
from jax.experimental import pallas as pl
from jax.experimental.pallas import tpu as pltpu
from jax.sharding import PartitionSpec as P

TB = 128
K = 64
PB = 32
ITERS = 2
HW = 8
NZ = 8
NX = 4
NY = 4
N_DOM = 32
N_COL = 8
TPD = 24
HTD = 8
NT = TPD + HTD
OWN = 4
EXT = PB + 2 * HW
HUBS = 32
HALF = 32
MESH = pl.DeviceIdType.MESH
F32 = jnp.float32
BF16 = jnp.bfloat16
HI = lax.Precision.HIGHEST


def wrap(value, count):
    return lax.rem(value + count, count)


def nn(a, b):
    return jnp.dot(a, b, precision=HI, preferred_element_type=F32)


def nt(a, b):
    return lax.dot_general(a, b, (((1,), (1,)), ((), ())), precision=HI, preferred_element_type=F32)


def split(value):
    high = value.astype(BF16)
    return high, (value - high.astype(F32)).astype(BF16)


def eliminate(matrix):
    full = (8, 2 * K)
    rows = lax.broadcasted_iota(jnp.int32, full, 0)
    lanes = lax.broadcasted_iota(jnp.int32, full, 1)
    wide = jnp.concatenate([matrix, jnp.zeros((K, K), F32)], axis=1)
    blocks = [jnp.where(lanes - K == rows + 8 * b, 1.0, wide[8 * b : 8 * b + 8]) for b in range(K // 8)]
    for home in range(K // 8):
        cols = [
            [jnp.broadcast_to(blocks[b][:, 8 * home + c : 8 * home + c + 1], full) for c in range(8)]
            for b in range(home, K // 8)
        ]
        work = [jnp.broadcast_to(blocks[home][r : r + 1, :], full) for r in range(8)]
        a = [[jnp.broadcast_to(cols[0][c][r : r + 1, :], full) for c in range(r + 1)] for r in range(8)]
        scale, done = [], []
        for c in range(8):
            scale.append(lax.rsqrt(a[c][c]))
            done.append(work[c] * scale[c])
            for r in range(c + 1, 8):
                a[r][c] = a[r][c] * scale[c]
            for r in range(c + 1, 8):
                for e in range(c + 1, r + 1):
                    a[r][e] = a[r][e] - a[r][c] * a[e][c]
                work[r] = work[r] - a[r][c] * done[c]
        back = [None] * 8
        for c in reversed(range(8)):
            value = done[c]
            for r in range(c + 1, 8):
                value = value - a[r][c] * back[r]
            back[c] = value * scale[c]
        for b in range(home + 1, K // 8):
            for c in range(8):
                blocks[b] = blocks[b] - cols[b - home][c] * back[c]
        for r in range(8):
            blocks[home] = jnp.where(rows == r, done[r], blocks[home])
    return jnp.concatenate(blocks, axis=0)[:, K:]


def plan(band_rows, band_cols, hub_rows, hub_slots):
    full = (NT, TB)
    sub = lax.broadcasted_iota(jnp.int32, full, 0)
    lane = lax.broadcasted_iota(jnp.int32, full, 1)
    key_s = jnp.zeros(full, jnp.int32)
    key_l = jnp.full(full, 4 * PB, jnp.int32)
    src_l = jnp.zeros(full, jnp.int32)
    for t in range(NT):
        key = band_rows[t] if t < TPD else PB + hub_rows[t - TPD]
        src = band_cols[t] if t < TPD else hub_slots[t - TPD]
        key_s = jnp.where(sub == t, key, key_s)
        key_l = jnp.where(lane == t, key, key_l)
        src_l = jnp.where(lane == t, src, src_l)

    def one(cond):
        return jnp.where(cond, 1, 0)

    same = jnp.where(sub < lane, one(key_s == key_l), 0)
    place = jnp.sum(one(key_s < key_l) + same, axis=0, keepdims=True)
    again = jnp.sum(same, axis=0, keepdims=True)
    place = jnp.where(lane < NT, jnp.broadcast_to(place, full), NT)
    chosen = one(place == sub)

    def across(value):
        return jnp.sum(value, axis=1, keepdims=True)

    columns = [
        across(chosen * lane),
        across(chosen * src_l),
        across(chosen * one(jnp.broadcast_to(again, full) > 0)),
        jnp.maximum(across(one(key_l <= sub)) - 1, 0),
        one(across(one(key_l == sub)) > 0),
        jnp.maximum(across(one(key_l <= sub + PB)) - 1, 0),
        one(across(one(key_l == sub + PB)) > 0),
    ]
    table = jnp.zeros(full, jnp.int32)
    for n, column in enumerate(columns):
        table = jnp.where(lane == n, jnp.broadcast_to(column, full), table)
    return table


def kernel(
    blocks_hbm, rows_hbm, cols_hbm, hrows_hbm, slots_hbm, vec_hbm, dir_hbm, rot_hbm, band_hbm, hub_hbm,
    mix_out, xt2, ritz_out,
    hub_blocks, band_rows, band_cols, hub_rows, hub_slots,
    tiles, weights, table_v, table, rot, xt,
    own, cand, hca, hubz, eb0, eb1, eb2, eh0, eh1, eh2, pr0, pr1, pr2, mixed,
    ssend, srecv, rsum, rrecv, pay0, ra0, rb0, rx0, rc0, pay1, ra1, rb1, rx1, rc1,
    wpay, wrecv, wplane, wz, wend, lsem, ssem, rsem,
):
    d = lax.axis_index("dom")
    q = lax.axis_index("col")
    x, z = d // NZ, d % NZ
    y, c = q // 2, q % 2
    other = 1 - c
    sib = (d, q + 1 - 2 * c)
    band, hub, prods = (eb0, eb1, eb2), (eh0, eh1, eh2), (pr0, pr1, pr2)

    def at_y(k):
        return (d, 2 * wrap(y + k, NY) + c)

    def at_xz(i, k):
        return (wrap(x + i, NX) * NZ + wrap(z + k, NZ), q)

    def at_xy(i, k):
        return (wrap(x + i, NX) * NZ + z, 2 * wrap(y + k, NY) + c)

    plane = ((2, 2), (2, 1), (2, 3), (1, 2), (3, 2), (2, 0), (0, 2), (1, 1), (1, 3), (3, 1), (3, 3), (1, 0), (3, 0), (0, 1), (0, 3))
    partners = [at_xz(0, k) for k in (4, 3, 5, 2, 6, 1, 7)] + [at_xz(i, 0) for i in (2, 1, 3)]
    partners += [(wrap(d + 1, N_DOM), q), (wrap(d - 1, N_DOM), q)] + [(d, wrap(q + k, N_COL)) for k in range(1, N_COL)]

    barrier = pltpu.get_barrier_semaphore()
    for partner in partners:
        pl.semaphore_signal(barrier, inc=1, device_id=partner, device_id_type=MESH)

    local = []
    for n, (src, dst) in enumerate(
        (
            (blocks_hbm, hub_blocks),
            (vec_hbm, xt.at[pl.ds(0, K)]),
            (rows_hbm, band_rows),
            (cols_hbm, band_cols),
            (hrows_hbm, hub_rows),
            (slots_hbm, hub_slots),
            (dir_hbm, xt.at[pl.ds(K, K)]),
            (band_hbm, tiles.at[pl.ds(0, TPD)]),
            (hub_hbm, tiles.at[pl.ds(TPD, HTD)]),
            (rot_hbm, rot),
        )
    ):
        local.append(pltpu.make_async_copy(src, dst, lsem.at[n]))
        local[n].start()
    counter = [0]
    pending = []

    def sems(n=1):
        counter[0] += n
        return counter[0] - n

    def drain():
        for item in pending:
            if isinstance(item, tuple):
                ref, sem = item
                pltpu.make_async_copy(ref, ref, ssem.at[sem]).wait()
            else:
                item.wait_send()
        pending.clear()

    def send(src, dst, sem, device):
        copy = pltpu.make_async_remote_copy(
            src_ref=src, dst_ref=dst, send_sem=ssem.at[sem], recv_sem=rsem.at[sem],
            device_id=device, device_id_type=MESH,
        )
        copy.start()
        return copy

    def arrived(ref, sem):
        pltpu.make_async_copy(ref, ref, rsem.at[sem]).wait()

    def block_of(col):
        return pl.ds(HW + OWN * col, OWN)

    local[0].wait()
    mask = [jnp.where(hub_blocks[d] - d * PB - q * OWN == j, 1.0, 0.0) for j in range(OWN)]
    names = ("ha", "p", "hb", "pf", "h", "hc", "hcf")
    gsem = [dict(zip(names, [sems(n) for n in (1, NY, NZ, NY, 4, NX, NX)])) for _ in range(3)]
    hub_row = jnp.clip(hub_blocks[d] - d * PB, 0, PB - 1)

    def g_start(g, ref, first):
        for j in range(OWN):
            block = ref[first : first + K, TB * j : TB * (j + 1)]
            own[g, j] = block
            band[g][HW + OWN * q + j] = block
        mine = band[g].at[block_of(q)]
        for k in (2, 1, 3):
            pending.append(send(own.at[g], mine, gsem[g]["p"] + k, at_y(k)))
        pending.append(send(own.at[g], mine, gsem[g]["p"], sib))

    def masked(ref, first):
        pick = jnp.zeros((K, TB), F32)
        for j in range(OWN):
            pick = pick + ref[first : first + K, TB * j : TB * (j + 1)] * mask[j]
        return pick

    def g_hub_start(g, term):
        cand[g] = term
        for k in range(1, N_COL):
            peer = wrap(q + k, N_COL)
            send(cand.at[g, pl.ds(HALF * (peer % 2), HALF)], hca.at[g, q], gsem[g]["ha"], (d, peer))
        pending.append((hca.at[g, pl.ds(0, N_COL - 1)], gsem[g]["ha"]))
        hca[g, q] = cand[g, pl.ds(HALF * c, HALF)]

    def g_hub(g, base=None):
        arrived(hca.at[g, pl.ds(0, N_COL - 1)], gsem[g]["ha"])
        piece = hca[g, 0]
        for k in range(1, N_COL):
            piece = piece + hca[g, k]
        hubz[g, z] = piece if base is None else base - piece
        for k in (4, 3, 5, 2, 6, 1, 7):
            pending.append(send(hubz.at[g, z], hubz.at[g, z], gsem[g]["hb"] + k, at_xz(0, k)))
        hub_on(g, z)

    def g_panel(g):
        for k in (1, 3, 2):
            block = band[g].at[block_of(2 * wrap(y - k, NY) + c)]
            arrived(block, gsem[g]["p"] + k)
            pending.append(send(block, block, gsem[g]["pf"] + k, sib))
        low, high = band[g].at[pl.ds(OWN * c, OWN)], band[g].at[pl.ds(HW + PB + OWN * c, OWN)]
        pending.append(send(band[g].at[block_of(N_COL - 2 + c)], low, gsem[g]["h"], (wrap(d + 1, N_DOM), q)))
        pending.append(send(band[g].at[block_of(c)], high, gsem[g]["h"] + 1, (wrap(d - 1, N_DOM), q)))

    def slab(g, at_x, half):
        return hub[g].at[pl.ds(NZ * at_x, NZ), pl.ds(HALF * half, HALF)]

    def hub_on(g, at_z):
        mine = hub[g].at[NZ * x + at_z, pl.ds(HALF * c, HALF)]
        for i in (2, 1, 3):
            send(hubz.at[g, at_z], mine, gsem[g]["hc"] + i, at_xz(i, 0))
        hub[g][NZ * x + at_z, pl.ds(HALF * c, HALF)] = hubz[g, at_z]

    def g_spread(g, part=None):
        near = (1, 7, 2, 6), (3, 5, 4)
        for k in near[0] + near[1] if part is None else near[part]:
            at_z = wrap(z - k, NZ)
            arrived(hubz.at[g, at_z], gsem[g]["hb"] + k)
            hub_on(g, at_z)
        if part != 0:
            pending.extend((hubz.at[g], gsem[g]["hc"] + i) for i in (1, 2, 3))
            pending.append(send(hubz.at[g], slab(g, x, c), gsem[g]["hcf"], sib))

    def g_halo(g):
        for n, at in enumerate((OWN * c, HW + PB + OWN * c)):
            part = band[g].at[pl.ds(at, OWN)]
            arrived(part, gsem[g]["h"] + n)
            pending.append(send(part, part, gsem[g]["h"] + 2 + n, sib))

    def g_panel_end(g):
        arrived(band[g].at[block_of(2 * y + other)], gsem[g]["p"])
        for k in (1, 3, 2):
            arrived(band[g].at[block_of(2 * wrap(y - k, NY) + other)], gsem[g]["pf"] + k)

    def g_halo_end(g):
        arrived(band[g].at[pl.ds(OWN * other, OWN)], gsem[g]["h"] + 2)
        arrived(band[g].at[pl.ds(HW + PB + OWN * other, OWN)], gsem[g]["h"] + 3)

    def g_pass(g):
        for i in (1, 3, 2):
            part = slab(g, wrap(x - i, NX), c)
            arrived(part, gsem[g]["hc"] + i)
            pending.append(send(part, part, gsem[g]["hcf"] + i, sib))

    def g_hub_end(g):
        for i in (0, 1, 3, 2):
            arrived(slab(g, wrap(x - i, NX), other), gsem[g]["hcf"] + i)

    def multiply(g, source, first, count):
        def group(n, total):
            for u in range(8):
                t = first + 8 * n + u
                high, low = split(source[table[t, 1]])
                left = jnp.concatenate(
                    [jnp.concatenate([high, high], axis=1), jnp.concatenate([low, jnp.zeros_like(low)], axis=1)], axis=0
                )
                both = jnp.dot(left, weights[table[t, 0]], preferred_element_type=F32)
                product = both[:K] + both[K:]
                total = total * table[t, 2].astype(F32) + product
                prods[g][t] = total
            return total

        lax.fori_loop(0, count // 8, group, jnp.zeros((K, TB), F32))

    def row_sum(g, r):
        return prods[g][table[r, 3]] * table[r, 4].astype(F32) + prods[g][table[r, 5]] * table[r, 6].astype(F32)

    ssems = [(sems(NY), sems(NY)) for _ in range(ITERS)]

    def scatter_start(n, rows_of, between=None):
        for k in (2, 1, 3, 0):
            for j, block in enumerate(rows_of(OWN * (2 * wrap(y + k, NY) + other))):
                ssend[n, k, j] = block
            pending.append(send(ssend.at[n, k], srecv.at[n, k], ssems[n][0] + k, sib))
        if between is not None:
            between()
        for k in (2, 1, 3):
            blocks = rows_of(OWN * (2 * wrap(y + k, NY) + c))
            arrived(srecv.at[n, k], ssems[n][0] + k)
            for j, block in enumerate(blocks):
                rsum[n, k, j] = block + srecv[n, k, j]
            pending.append(send(rsum.at[n, k], rrecv.at[n, k], ssems[n][1] + k, at_y(k)))
        return rows_of(OWN * q)

    def scatter_end(n, blocks):
        arrived(srecv.at[n, 0], ssems[n][0])
        blocks = [block + srecv[n, 0, j] for j, block in enumerate(blocks)]
        for k in (1, 3, 2):
            arrived(rrecv.at[n, k], ssems[n][1] + k)
            blocks = [block + rrecv[n, k, j] for j, block in enumerate(blocks)]
        return jnp.concatenate(blocks, axis=1)

    def cross_of(blocks, groups, at):
        highs, lows = zip(*[split(block) for block in blocks])
        there = [split(jnp.concatenate([band[g][HW + r] for g in groups], axis=0)) for r in at]
        left, right = [], []
        for ph, pl_, (gh, gl) in zip(highs, lows, there):
            left += [ph, ph, pl_]
            right += [gh, gl, gh]
        return lax.dot_general(
            jnp.concatenate(left, axis=1), jnp.concatenate(right, axis=1), (((1,), (1,)), ((), ())),
            preferred_element_type=F32,
        )

    def panel_cross(block_at, groups):
        def some(n, total):
            for u in range(0, 4, 2):
                at = (4 * n + u, 4 * n + u + 1)
                total = total + cross_of([block_at(r) for r in at], groups, at)
            return total

        return lax.fori_loop(0, PB // 4, some, jnp.zeros((K, K * len(groups)), F32))

    sets = ((pay0, ra0, rb0, rx0, rc0), (pay1, ra1, rb1, rx1, rc1))
    asems = [sems(4) for _ in range(ITERS + 1)]

    def refs(n):
        return [(ref.at[0] if n == 0 else ref.at[n - 1]) for ref in sets[min(n, 1)]]

    def a_start(n, value):
        pay, ra, _, _, _ = refs(n)
        pay[...] = value
        for k in range(1, N_COL):
            peer = wrap(q + k, N_COL)
            send(pay.at[pl.ds(8 * peer, 8)], ra.at[q], asems[n], (d, peer))
        pending.append((ra.at[pl.ds(0, N_COL - 1)], asems[n]))
        ra[q] = pay[pl.ds(8 * q, 8)]

    def a_sum(ref, count, sem):
        arrived(ref.at[pl.ds(0, count - 1)], sem)
        total = ref[0]
        for k in range(1, count):
            total = total + ref[k]
        return total

    def a_z(n):
        _, ra, rb, _, _ = refs(n)
        rb[z] = a_sum(ra, N_COL, asems[n])
        for k in (4, 3, 5, 2, 6, 1, 7):
            send(rb.at[z], rb.at[z], asems[n] + 1, at_xz(0, k))
        pending.append((rb.at[pl.ds(0, NZ - 1)], asems[n] + 1))

    def a_x(n):
        _, _, rb, rx, _ = refs(n)
        rx[x] = a_sum(rb, NZ, asems[n] + 1)
        for i in (2, 1, 3):
            send(rx.at[x], rx.at[x], asems[n] + 2, at_xz(i, 0))
        pending.append((rx.at[pl.ds(0, NX - 1)], asems[n] + 2))

    def a_back(n):
        _, _, _, rx, rc = refs(n)
        rc[q] = a_sum(rx, NX, asems[n] + 2)
        for k in range(1, N_COL):
            send(rc.at[q], rc.at[q], asems[n] + 3, (d, wrap(q + k, N_COL)))
        pending.append((rc.at[pl.ds(0, N_COL - 1)], asems[n] + 3))

    def a_end(n):
        _, _, _, _, rc = refs(n)
        arrived(rc.at[pl.ds(0, N_COL - 1)], asems[n] + 3)
        return jnp.concatenate([rc[k] for k in range(N_COL)], axis=0)

    wsems = [sems(4) for _ in range(ITERS)]

    def w_start(n, w):
        square = nt(w, w)
        wpay[n] = jnp.concatenate([square[: K // 2], square[K // 2 :]], axis=1)
        pending.append(send(wpay.at[n, pl.ds(16 * other, 16)], wrecv.at[n], wsems[n], sib))

    def w_plane(n):
        arrived(wrecv.at[n], wsems[n])
        at = x * NY + y
        wplane[n, at] = wpay[n, pl.ds(16 * c, 16)] + wrecv[n]
        for i, k in plane:
            send(wplane.at[n, at], wplane.at[n, at], wsems[n] + 1, at_xy(i, k))
        pending.append((wplane.at[n, pl.ds(0, NX * NY - 1)], wsems[n] + 1))

    def w_z(n):
        wz[n, z] = a_sum(wplane.at[n], NX * NY, wsems[n] + 1)
        for k in (4, 3, 5, 2, 6, 1, 7):
            send(wz.at[n, z], wz.at[n, z], wsems[n] + 2, at_xz(0, k))
        pending.append((wz.at[n, pl.ds(0, NZ - 1)], wsems[n] + 2))

    def w_back(n):
        wend[n, pl.ds(16 * c, 16)] = a_sum(wz.at[n], NZ, wsems[n] + 2)
        half = wend.at[n, pl.ds(16 * c, 16)]
        pending.append(send(half, half, wsems[n] + 3, sib))

    def w_end(n):
        arrived(wend.at[n, pl.ds(16 * other, 16)], wsems[n] + 3)
        whole = wend[n]
        return jnp.concatenate([whole[:, :K], whole[:, K:]], axis=0)

    def prepared(it, gvd, cross):
        coeff = rot[it]
        c1, c2, c3 = coeff[:, 0:K], coeff[:, K : 2 * K], coeff[:, 2 * K :]
        shift = nn(c2, cross[:, :K])
        yall = jnp.concatenate([c1 - shift, c3, c2], axis=1)
        zall = jnp.concatenate([-shift, c3, c2], axis=1)
        upper = jnp.concatenate([gvd, cross], axis=0)
        return yall, zall, upper, nn(yall, upper)

    def coefficients(yall, zall, left, lower):
        reduced = nt(jnp.concatenate([left, nt(yall, lower)], axis=1), yall)
        inverse = eliminate(reduced)
        return jnp.concatenate([nn(inverse, yall), nn(inverse, zall)], axis=0)

    def prepare(t, carry):
        high, low = split(tiles[t].T)
        weights[t, 0:TB] = high
        weights[t, TB:] = low
        return carry

    def prepare_some(n):
        lax.fori_loop(NT // 4 * n, NT // 4 * (n + 1), prepare, 0)

    local[1].wait()
    pl.semaphore_wait(barrier, len(partners))
    g_hub_start(0, masked(xt, 0))
    g_start(0, xt, 0)
    local[6].wait()
    both = xt[0 : 2 * K, :]
    gram = nt(both, both)
    a_start(0, jnp.concatenate([gram[:K], gram[K:]], axis=1))
    for n in (2, 3, 4, 5):
        local[n].wait()
    table_v[...] = plan(band_rows, band_cols, hub_rows, hub_slots)
    to_smem = pltpu.make_async_copy(table_v, table, lsem.at[10])
    to_smem.start()
    for n in (7, 8, 9):
        local[n].wait()
    prepare_some(0)
    g_hub(0)
    prepare_some(1)
    a_z(0)
    g_panel(0)
    g_spread(0, 0)
    g_hub_start(1, masked(xt, K))
    g_start(1, xt, K)
    prepare_some(2)
    g_spread(0, 1)
    a_x(0)
    to_smem.wait()
    g_halo(0)
    g_panel_end(0)
    g_halo_end(0)
    multiply(0, band[0], 0, TPD)
    prepare_some(3)
    g_pass(0)
    g_hub(1)
    g_panel(1)
    a_back(0)
    g_hub_end(0)
    multiply(0, hub[0], TPD, HTD)

    def first_rows(r):
        return [row_sum(0, r + j) for j in range(OWN)]

    kept = scatter_start(0, first_rows, lambda: g_hub_start(2, row_sum(0, hub_row)))
    g_panel_end(1)
    crossed = panel_cross(lambda r: row_sum(0, r), (0, 1))
    g_hub(2, hub[0][d, pl.ds(HALF * c, HALF)])
    a_start(1, crossed)
    g_spread(1)
    g_halo(1)
    sums = a_end(0)
    gvd = jnp.concatenate([sums[:, : 2 * K], sums[:, 2 * K :]], axis=0)
    a_z(1)
    g_spread(2, 0)
    w = xt[0:K] - scatter_end(0, kept)
    xt[2 * K :] = w
    w_start(0, w)
    g_start(2, xt, 2 * K)
    w_plane(0)
    g_spread(2, 1)
    g_halo_end(1)
    multiply(1, band[1], 0, TPD)
    a_x(1)
    g_pass(1)
    g_hub_end(1)
    multiply(1, hub[1], TPD, HTD)
    a_back(1)
    w_z(0)
    g_panel(2)
    cross = gvd[:K] - a_end(1)
    yall, zall, upper, left = prepared(0, gvd, cross)
    w_back(0)
    g_pass(2)
    g_halo(2)
    lower = jnp.concatenate([cross, w_end(0)], axis=1)
    mix = coefficients(yall, zall, left, lower)
    mix_high, mix_low = split(mix[:K])
    mix_both = jnp.concatenate([mix_high, mix_low], axis=0)
    g_panel_end(2)
    g_halo_end(2)
    multiply(2, band[2], 0, TPD)
    g_hub_end(2)
    multiply(2, hub[2], TPD, HTD)

    def second_rows(r):
        stack = jnp.concatenate(
            [jnp.concatenate([row_sum(g, r + j) for j in range(OWN)], axis=1) for g in range(3)], axis=0
        )
        high, low = split(stack)
        one = jnp.dot(mix_both, high, preferred_element_type=F32)
        two = jnp.dot(mix_high, low, preferred_element_type=F32)
        out = one[:K] + one[K:] + two
        blocks = [out[:, TB * j : TB * (j + 1)] for j in range(OWN)]
        for j in range(OWN):
            mixed[r + j] = blocks[j]
        return blocks

    kept = scatter_start(1, second_rows)
    a_start(2, nt(panel_cross(lambda r: mixed[r], (0, 1, 2)), mix[:, : K * 3]))
    xt2[0 : 2 * K] = nn(mix, xt[...])
    carried = jnp.concatenate([nn(mix, upper), nt(mix, lower)], axis=1)
    gvd = nt(carried, mix)
    drain()
    a_z(2)
    w = xt2[0:K] - scatter_end(1, kept)
    xt2[2 * K :] = w
    w_start(1, w)
    w_plane(1)
    a_x(2)
    w_z(1)
    a_back(2)
    w_back(1)
    cross = gvd[:K] - a_end(2)
    ritz_out[...] = cross[:, :K]
    yall, zall, upper, left = prepared(1, gvd, cross)
    drain()
    mix_out[...] = coefficients(yall, zall, left, jnp.concatenate([cross, w_end(1)], axis=1))

    drain()


def finish(mix, state, ritz, vec_out, dir_out, ritz_out):
    whole = state[...]
    vec_out[...] = nn(mix[:K], whole)
    dir_out[...] = nn(mix[K:], whole)
    ritz_out[...] = ritz[...].T


def per_device(
    band_tiles, band_rows, band_cols, hub_tiles, hub_rows, hub_slots, hub_blocks,
    start_vectors, prior_directions, rotation,
):
    vmem = pl.BlockSpec(memory_space=pltpu.VMEM)
    hbm = pl.BlockSpec(memory_space=pltpu.HBM)
    rows = start_vectors.shape[0]
    ext = [pltpu.VMEM((EXT, K, TB), F32)] * 3 + [pltpu.VMEM((HUBS, K, TB), F32)] * 3
    mix, state, ritz = pl.pallas_call(
        kernel,
        out_shape=(
            jax.ShapeDtypeStruct((2 * K, 3 * K), F32),
            jax.ShapeDtypeStruct((3 * K, rows), F32),
            jax.ShapeDtypeStruct((K, K), F32),
        ),
        in_specs=[hbm] * 10,
        out_specs=(vmem, vmem, vmem),
        scratch_shapes=[
            *[pltpu.SMEM((count,), jnp.int32) for count in (HUBS, TPD, TPD, HTD, HTD)],
            pltpu.VMEM((NT, TB, TB), F32),
            pltpu.VMEM((NT, 2 * TB, TB), BF16),
            pltpu.VMEM((NT, TB), jnp.int32),
            pltpu.SMEM((NT, TB), jnp.int32),
            pltpu.VMEM((ITERS, K, 3 * K), F32),
            pltpu.VMEM((3 * K, rows), F32),
            pltpu.VMEM((3, OWN, K, TB), F32),
            pltpu.VMEM((3, K, TB), F32),
            pltpu.VMEM((3, N_COL, HALF, TB), F32),
            pltpu.VMEM((3, NZ, HALF, TB), F32),
            *ext,
            *[pltpu.VMEM((NT, K, TB), F32)] * 3,
            pltpu.VMEM((PB, K, TB), F32),
            *[pltpu.VMEM((ITERS, NY, OWN, K, TB), F32)] * 4,
            *[
                pltpu.VMEM((count,) + shape + (width,), F32)
                for count, width in ((1, 4 * K), (ITERS, 2 * K))
                for shape in ((K,), (N_COL, 8), (NZ, 8), (NX, 8), (N_COL, 8))
            ],
            pltpu.VMEM((ITERS, K // 2, 2 * K), F32),
            pltpu.VMEM((ITERS, K // 4, 2 * K), F32),
            pltpu.VMEM((ITERS, NX * NY, K // 4, 2 * K), F32),
            pltpu.VMEM((ITERS, NZ, K // 4, 2 * K), F32),
            pltpu.VMEM((ITERS, K // 2, 2 * K), F32),
            pltpu.SemaphoreType.DMA((11,)),
            pltpu.SemaphoreType.DMA((128,)),
            pltpu.SemaphoreType.DMA((128,)),
        ],
        compiler_params=pltpu.CompilerParams(
            collective_id=0, has_side_effects=True, vmem_limit_bytes=56 * 1024 * 1024
        ),
        name="lobpcg",
    )(
        hub_blocks, band_rows, band_cols, hub_rows, hub_slots, start_vectors.T, prior_directions.T,
        jnp.transpose(rotation, (0, 2, 1)), band_tiles, hub_tiles,
    )
    vec, direc, ritz = pl.pallas_call(
        finish,
        out_shape=(
            jax.ShapeDtypeStruct((K, rows), F32),
            jax.ShapeDtypeStruct((K, rows), F32),
            jax.ShapeDtypeStruct((K, K), F32),
        ),
        in_specs=[vmem] * 3,
        out_specs=(vmem, vmem, vmem),
        name="finish",
    )(mix, state, ritz)
    return vec.T, direc.T, ritz


def solution(mesh):
    return jax.shard_map(
        per_device,
        mesh=mesh,
        in_specs=(
            P(("dom", "col"), None, None),
            P(("dom", "col")),
            P(("dom", "col")),
            P(("dom", "col"), None, None),
            P(("dom", "col")),
            P(("dom", "col")),
            P(),
            P(("dom", "col"), None),
            P(("dom", "col"), None),
            P(),
        ),
        out_specs=(P(("dom", "col"), None), P(("dom", "col"), None), P()),
        check_vma=False,
    )
```
